128 devices in a mesh: seq: 2 (over y_hi), dp: 64 (over y_lo, z, x, core).
Axes of the slice: x: 4, y: 4 (y_hi: 2, y_lo: 2; y = y_hi * 2 + y_lo), z: 4, core: 2. Of those that a mesh axis runs over, the one named last changes fastest.
Arguments:
- tokens: bfloat16 [16384, 1024], P(('seq', 'dp')), may hold values from -6 to 6
- ln1_gain: bfloat16 [1024], P('dp'), may hold values from 0.099609375 to 1.8984375
- ln1_bias: bfloat16 [1024], P('dp'), may hold values from -4 to 4
- ln2_gain: bfloat16 [1024], P('dp'), may hold values from 0.099609375 to 1.8984375
- ln2_bias: bfloat16 [1024], P('dp'), may hold values from -4 to 4
- qkv_weight: bfloat16 [1024, 3072], P('dp'), may hold values from -0.1875 to 0.1875
- qkv_bias: bfloat16 [3072], P('dp'), may hold values from -4 to 4
- dense_weight: bfloat16 [1024, 1024], P('dp'), may hold values from -1.5 to 1.5
- dense_bias: bfloat16 [1024], P('dp'), may hold values from -4 to 4
- fc_in_weight: bfloat16 [1024, 4096], P('dp'), may hold values from -0.1875 to 0.1875
- fc_in_bias: bfloat16 [4096], P('dp'), may hold values from -4 to 4
- fc_out_weight: bfloat16 [4096, 1024], P('dp'), may hold values from -0.09375 to 0.09375
- fc_out_bias: bfloat16 [1024], P('dp'), may hold values from -4 to 4
- out_grad: bfloat16 [16384, 1024], P(('seq', 'dp')), may hold values from -6 to 6
Outputs:
- mixed: bfloat16 [16384, 1024], P(('seq', 'dp'))
- tokens_grad: float32 [16384, 1024], P(('seq', 'dp'))
- ln1_gain_grad: float32 [1024], P('dp')
- ln1_bias_grad: float32 [1024], P('dp')
- ln2_gain_grad: float32 [1024], P('dp')
- ln2_bias_grad: float32 [1024], P('dp')
- qkv_weight_grad: float32 [1024, 3072], P('dp')
- qkv_bias_grad: float32 [3072], P('dp')
- dense_weight_grad: float32 [1024, 1024], P('dp')
- dense_bias_grad: float32 [1024], P('dp')
- fc_in_weight_grad: float32 [1024, 4096], P('dp')
- fc_in_bias_grad: float32 [4096], P('dp')
- fc_out_weight_grad: float32 [4096, 1024], P('dp')
- fc_out_bias_grad: float32 [1024], P('dp')
The draws below stay inside these ranges and needn't reach their ends.
All inputs are finite; a program needn't handle non-finite values.
Results may differ from the reference program's by a relative error of at most 0.011.
Values may be sent and summed in bfloat16 or wider, within the bound.
No kernel may reach another device: no remote copies, remote signals or barrier semaphores. Data moves between devices by JAX's collectives and lax.ppermute only.
A program may use at most 192 MiB of HBM per device.

```python
import jax
import jax.numpy as jnp
from jax import lax

D = 1024
HEADS = 16
HEAD_DIM = 64
ROT = 16
FF = 4096
TOK_DEV = 128
SEQLEN = 256
TOKENS = 16384
N_SEQ = 2
N_DP = 64


def shard_levels(rng, dims, split, low, largest):
    level, own = 1.0, jax.random.fold_in(rng, 6)
    for dim, shards_of in split:
        steps = jnp.exp(jax.random.uniform(jax.random.fold_in(own, dim), (shards_of,), jnp.float32, low / len(split), largest / len(split)))
        level = level * jnp.repeat(steps, dims[dim] // shards_of).reshape([-1 if axis == dim else 1 for axis in range(len(dims))])
    return level


def centred(rng, dims, spread, bound, split=(), dtype=jnp.bfloat16):
    values = spread * jax.random.normal(rng, dims, jnp.float32)
    if split:
        values = values * shard_levels(rng, dims, split, -0.22, 0.18)
    return jnp.clip(values, -bound, bound).astype(dtype)


def setup_inputs(seed: int = 0) -> dict:
    streams_of = jax.random.split(jax.random.key(seed), 15)
    return {
        "tokens": centred(streams_of[0], (TOKENS, D), 1.0, 6.0, ((0, 128),)),
        "ln1_gain": jnp.clip(1.0 + 0.18 * jax.random.normal(streams_of[1], (D,), jnp.float32), 0.099609375, 1.8984375).astype(jnp.bfloat16),
        "ln1_bias": centred(streams_of[2], (D,), 0.3, 4.0, ((0, 64),)),
        "ln2_gain": jnp.clip(1.0 + 0.18 * jax.random.normal(streams_of[3], (D,), jnp.float32), 0.099609375, 1.8984375).astype(jnp.bfloat16),
        "ln2_bias": centred(streams_of[4], (D,), 0.3, 4.0, ((0, 64),)),
        "qkv_weight": centred(streams_of[5], (D, 3 * D), D ** -0.5, 0.1875, ((0, 64),)),
        "qkv_bias": centred(streams_of[6], (3 * D,), 0.3, 4.0, ((0, 64),)),
        "dense_weight": centred(streams_of[7], (D, D), (max(1, 4 * D // SEQLEN)) ** -0.5, 1.5, ((0, 64),)),
        "dense_bias": centred(streams_of[8], (D,), 0.3, 4.0, ((0, 64),)),
        "fc_in_weight": centred(streams_of[9], (D, FF), D ** -0.5, 0.1875, ((0, 64),)),
        "fc_in_bias": centred(streams_of[10], (FF,), 0.3, 4.0, ((0, 64),)),
        "fc_out_weight": centred(streams_of[11], (FF, D), FF ** -0.5, 0.09375, ((0, 64),)),
        "fc_out_bias": centred(streams_of[12], (D,), 0.3, 4.0, ((0, 64),)),
        "out_grad": centred(streams_of[13], (TOKENS, D), 1.0, 6.0, ((0, 128),)),
    }


@jax.custom_vjp
def low(v):
    return lax.optimization_barrier(v.astype(jnp.bfloat16)).astype(jnp.float32)

@jax.custom_vjp
def low_back(v):
    return v

def low_keep(v):
    return (low(v), None)

def low_pass(kept, grad):
    return (grad,)

def back_keep(v):
    return (v, None)

def back_low(kept, grad):
    return (low(grad),)
low.defvjp(low_keep, low_pass)
low_back.defvjp(back_keep, back_low)
epsilon = 1e-05
highest = lax.Precision.HIGHEST

def layer_norm(values, gain, shift):
    average = lax.optimization_barrier(jnp.mean(values, axis=-1, keepdims=True))
    centered = values - average
    variance = lax.optimization_barrier(jnp.mean(centered * centered, axis=-1, keepdims=True))
    return centered * lax.rsqrt(variance + epsilon) * gain + shift

def rotary_tables(positions):
    halves = jnp.arange(ROT // 2).astype(jnp.float32)
    frequency = jnp.power(10000.0, -2.0 * halves / ROT)
    angles = positions.astype(jnp.float32)[:, None] * frequency[None, :]
    angles = jnp.concatenate([angles, angles], axis=1)
    return (jnp.cos(angles), jnp.sin(angles))

def rotate(heads_in, cosine, sine):
    half_rot = ROT // 2
    first = heads_in[..., :half_rot]
    second = heads_in[..., half_rot:ROT]
    turned = jnp.concatenate([-second, first], axis=-1)
    moved = heads_in[..., :ROT] * cosine[:, None, :] + turned * sine[:, None, :]
    return jnp.concatenate([moved, heads_in[..., ROT:]], axis=-1)

def forward(params, inputs):
    gain_one, bias_one, gain_two, bias_two, qkv_w, qkv_b, dense_w, dense_b, in_w, in_b, out_w, out_b = params
    length = inputs.shape[0]
    normed_one = low(layer_norm(inputs, gain_one, bias_one))
    normed_two = low(layer_norm(inputs, gain_two, bias_two))
    projected = low_back(jnp.dot(normed_one, qkv_w, precision=highest) + qkv_b)
    projected = projected.reshape(length, 3, HEADS, HEAD_DIM)
    cosine, sine = rotary_tables(jnp.arange(length))
    queries = low(low_back(rotate(projected[:, 0], cosine, sine)))
    keys = low(low_back(rotate(projected[:, 1], cosine, sine)))
    values = low(low_back(projected[:, 2]))
    scores = jnp.einsum('qhd,khd->hqk', queries, keys, precision=highest) * HEAD_DIM ** (-0.5)
    scores = low_back(scores)
    positions = jnp.arange(length)
    allowed = positions[:, None] >= positions[None, :]
    scores = jnp.where(allowed[None], scores, -1e+30)
    probs = low(jax.nn.softmax(scores, axis=-1))
    attended = jnp.einsum('hqk,khd->qhd', probs, values, precision=highest)
    attended = low(low_back(attended.reshape(length, D)))
    attn_out = jnp.dot(attended, dense_w, precision=highest) + dense_b
    hidden_pre = low_back(jnp.dot(normed_two, in_w, precision=highest) + in_b)
    active = low(jax.nn.gelu(hidden_pre, approximate=False))
    mlp_out = jnp.dot(active, out_w, precision=highest) + out_b
    return inputs + attn_out + mlp_out

def reference(tokens, ln1_gain, ln1_bias, ln2_gain, ln2_bias, qkv_weight, qkv_bias, dense_weight, dense_bias, fc_in_weight, fc_in_bias, fc_out_weight, fc_out_bias, out_grad):
    params = tuple((item.astype(jnp.float32) for item in (ln1_gain, ln1_bias, ln2_gain, ln2_bias, qkv_weight, qkv_bias, dense_weight, dense_bias, fc_in_weight, fc_in_bias, fc_out_weight, fc_out_bias)))

    def arrange(array):
        return array.reshape(N_SEQ, N_DP, TOK_DEV, D).transpose(1, 0, 2, 3).reshape(N_DP, N_SEQ * TOK_DEV, D)

    def restore(array):
        return array.reshape(N_DP, N_SEQ, TOK_DEV, D).transpose(1, 0, 2, 3).reshape(N_SEQ * N_DP * TOK_DEV, D)
    inputs = arrange(tokens).astype(jnp.float32)
    cotangents = arrange(out_grad).astype(jnp.float32)

    def per_sequence(totals, pair):
        sequence, cotangent = pair
        result, pullback = jax.vjp(forward, params, sequence)
        grads, input_grad = pullback(cotangent)
        totals = tuple((left + right for left, right in zip(totals, grads)))
        return (totals, (result.astype(jnp.bfloat16), input_grad))
    zeros = tuple((jnp.zeros_like(item) for item in params))
    totals, (outputs, input_grads) = lax.scan(per_sequence, zeros, (inputs, cotangents))
    return (restore(outputs), restore(input_grads), totals[0], totals[1], totals[2], totals[3], totals[4], totals[5], totals[6], totals[7], totals[8], totals[9], totals[10], totals[11])
```

```python
import functools

import jax
import jax.numpy as jnp
from jax import lax
from jax.experimental import pallas as pl
from jax.experimental.pallas import tpu as pltpu
from jax.sharding import Mesh
from jax.sharding import PartitionSpec as P

HEADS = 16
HEAD_DIM = 64
ROT = 16
WIDTH = 1024
FF = 4096
TOK = 128
F32 = jnp.float32
BF16 = jnp.bfloat16
EPSILON = 1e-05
AXES = ("s", "yl", "z", "x", "c")
RING_Y = ("s", "yl")
GROUP = ("s", "yl", "c")
QKV = 384
HID = 512
VMEM_LIMIT = 48 * 1024 * 1024


def shift(values, axis, step):
    return lax.ppermute(values, axis, [(i, (i + step) % 4) for i in range(4)])


def swap_core(values):
    return lax.ppermute(values, "c", [(0, 1), (1, 0)])


def exchange(values, axes, count, mask):
    return lax.ppermute(values, axes, [(i, i ^ mask) for i in range(count)])


def ring_gather(block, axis, dim):
    one = shift(block, axis, 1)
    three = shift(block, axis, -1)
    half = block.shape[dim] // 2
    low = lax.slice_in_dim(one, 0, half, axis=dim)
    high = lax.slice_in_dim(three, half, 2 * half, axis=dim)
    two = jnp.concatenate([shift(low, axis, 1), shift(high, axis, -1)], axis=dim)
    return [block, one, two, three]


def ring_scatter(blocks, axis, dim):
    own, one, two, three = blocks
    half = two.shape[dim] // 2
    low = shift(lax.slice_in_dim(two, 0, half, axis=dim).astype(BF16), axis, 1)
    high = shift(lax.slice_in_dim(two, half, 2 * half, axis=dim).astype(BF16), axis, -1)
    three_low = lax.slice_in_dim(three, 0, half, axis=dim).astype(F32) + low.astype(F32)
    three_high = lax.slice_in_dim(three, half, 2 * half, axis=dim).astype(F32)
    one_low = lax.slice_in_dim(one, 0, half, axis=dim).astype(F32)
    one_high = lax.slice_in_dim(one, half, 2 * half, axis=dim).astype(F32) + high.astype(F32)
    three = jnp.concatenate([three_low.astype(BF16), three_high.astype(BF16)], axis=dim)
    one = jnp.concatenate([one_low.astype(BF16), one_high.astype(BF16)], axis=dim)
    right = shift(three, axis, 1)
    left = shift(one, axis, -1)
    return own.astype(F32) + right.astype(F32) + left.astype(F32)


def smem():
    return pl.BlockSpec(memory_space=pltpu.SMEM)


def vmem():
    return pl.BlockSpec(memory_space=pltpu.VMEM)


def call(body, out_shape, operands, flops=0, size=1 << 20):
    return pl.pallas_call(
        body,
        out_shape=out_shape,
        in_specs=[smem()] + [vmem()] * (len(operands) - 1),
        out_specs=jax.tree.map(lambda _: vmem(), out_shape),
        compiler_params=pltpu.CompilerParams(vmem_limit_bytes=VMEM_LIMIT),
        cost_estimate=pl.CostEstimate(flops=flops, bytes_accessed=size, transcendentals=0),
    )(*operands)


def pack_body(at, qkv, small, fc_in, qs_out, in_out):
    rank = at[5]
    for d in range(4):
        target = lax.bitwise_xor(rank, d)
        for part in range(3):
            start = pl.multiple_of(part * WIDTH + target * 128, 128)
            qs_out[d, :, part * 128 : part * 128 + 128] = qkv[:, pl.ds(start, 128)]
        qs_out[d, :, QKV:] = small[...]
        in_out[d] = fc_in[:, pl.ds(pl.multiple_of(target * HID, HID), HID)]


def row_block(at, rz, rx, d):
    z = lax.rem(at[2] + 4 - rz, 4)
    x = lax.rem(at[3] + 4 - rx, 4)
    pair = lax.bitwise_xor(at[1] * 2 + at[4], d)
    yl, c = lax.div(pair, 2), lax.rem(pair, 2)
    return pl.multiple_of((((yl * 4 + z) * 4 + x) * 2 + c) * 16, 16)


def rows_in_body(at, b0, b1, b2, b3, out):
    for rx, block in enumerate((b0, b1, b2, b3)):
        for rz in range(4):
            for d in range(4):
                out[pl.ds(row_block(at, rz, rx, d), 16), :] = block[rz, d]


def rows_out_body(at, values, b0, b1, b2, b3):
    for rx, block in enumerate((b0, b1, b2, b3)):
        for rz in range(4):
            for d in range(4):
                block[rz, d] = values[pl.ds(row_block(at, rz, rx, d), 16), :]


def tail_place(at, rz, rx):
    z = lax.rem(at[2] + 4 - rz, 4)
    x = lax.rem(at[3] + 4 - rx, 4)
    place = z * 4 + x
    return lax.div(place, 2), pl.multiple_of(lax.rem(place, 2) * 512, 512)


def tail_in_body(at, b0, b1, b2, b3, out):
    for rz, block in enumerate((b0, b1, b2, b3)):
        for rx in range(4):
            k, lane = tail_place(at, rz, rx)
            out[pl.ds(pl.multiple_of(k * 16, 16), 16), pl.ds(lane, 512)] = block[rx, 0:16, :]
            out[pl.ds(pl.multiple_of(128 + k * 64, 16), 64), pl.ds(lane, 512)] = block[rx, 16:80, :]


def tail_out_body(at, values, b0, b1, b2, b3):
    for rz, block in enumerate((b0, b1, b2, b3)):
        for rx in range(4):
            k, lane = tail_place(at, rz, rx)
            block[rx, 0:16, :] = values[pl.ds(pl.multiple_of(k * 16, 16), 16), pl.ds(lane, 512)]
            block[rx, 16:80, :] = values[pl.ds(pl.multiple_of(128 + k * 64, 16), 64), pl.ds(lane, 512)]


def owner_body(at, *refs):
    qs, hidden = refs[0:8], refs[8:16]
    qkv_out, in_out, small_out = refs[16:]
    rank = at[5]
    small = jnp.zeros((16, 128), F32)
    for e in range(8):
        source = lax.bitwise_xor(rank, e)
        for part in range(3):
            start = pl.multiple_of(part * WIDTH + source * 128, 128)
            qkv_out[:, pl.ds(start, 128)] = qs[e][:, part * 128 : part * 128 + 128].astype(F32)
        small = small + qs[e][:, QKV:].astype(F32)
        in_out[:, pl.ds(pl.multiple_of(source * HID, HID), HID)] = hidden[e][...].astype(F32)
    small_out[...] = small


def attention_body(at, proj, grad, cos, sin_low, sin_high, out, dproj):
    parity = lax.rem(pl.program_id(0), 2)
    first_y = lax.rem(at[0] * 2 + at[1] + 4 - parity, 4)
    first = lax.div(first_y, 2)
    row = lax.broadcasted_iota(jnp.int32, (256, 256), 0)
    col = lax.broadcasted_iota(jnp.int32, (256, 256), 1)

    def place(index):
        block = jnp.where(index < 128, first, 1 - first)
        return lax.bitwise_and(index, 127) + 128 * block

    allowed = place(row) >= place(col)
    c, low, high = cos[...], sin_low[...], sin_high[...]

    def turn(values, sign):
        back = pltpu.roll(values, 128 - 8, 1)
        ahead = pltpu.roll(values, 8, 1)
        return values * c + sign * (back * low + ahead * high)

    queries = turn(proj[:, 0:128], 1.0).astype(BF16)
    keys = turn(proj[:, 128:256], 1.0).astype(BF16)
    values = proj[:, 256:384].astype(BF16)
    cot = grad[...]
    outs, dqs, dks, dvs = [], [], [], []
    nt = (((1,), (1,)), ((), ()))
    tn = (((0,), (0,)), ((), ()))
    scale = HEAD_DIM ** (-0.5)
    for h in range(2):
        lanes = slice(h * HEAD_DIM, (h + 1) * HEAD_DIM)
        q, k, v, g = queries[:, lanes], keys[:, lanes], values[:, lanes], cot[:, lanes]
        scores = lax.dot_general(q, k, nt, preferred_element_type=F32) * scale
        scores = jnp.where(allowed, scores, -1e30)
        peak = jnp.max(scores, axis=1, keepdims=True)
        weights = jnp.exp(scores - peak)
        probs = weights / jnp.sum(weights, axis=1, keepdims=True)
        rounded = probs.astype(BF16)
        outs.append(jnp.dot(rounded, v, preferred_element_type=F32))
        dprobs = lax.dot_general(g, v, nt, preferred_element_type=F32)
        inner = jnp.sum(probs * dprobs, axis=1, keepdims=True)
        ds = (probs * (dprobs - inner)).astype(BF16)
        dqs.append(jnp.dot(ds, k, preferred_element_type=F32) * scale)
        dks.append(lax.dot_general(ds, q, tn, preferred_element_type=F32) * scale)
        dvs.append(lax.dot_general(rounded, g, tn, preferred_element_type=F32))
    out[...] = jnp.concatenate(outs, axis=1).astype(BF16)
    dq = jnp.concatenate(dqs, axis=1).astype(BF16).astype(F32)
    dk = jnp.concatenate(dks, axis=1).astype(BF16).astype(F32)
    dproj[:, 0:128] = turn(dq, -1.0).astype(BF16)
    dproj[:, 128:256] = turn(dk, -1.0).astype(BF16)
    dproj[:, 256:384] = jnp.concatenate(dvs, axis=1).astype(BF16)


def attention(at, proj, grad, tables):
    table = pl.BlockSpec((256, 128), lambda i: (i % 2, 0))
    return pl.pallas_call(
        attention_body,
        grid=(4,),
        out_shape=(
            jax.ShapeDtypeStruct((1024, 128), BF16),
            jax.ShapeDtypeStruct((1024, QKV), BF16),
        ),
        in_specs=[
            smem(),
            pl.BlockSpec((256, QKV), lambda i: (i, 0)),
            pl.BlockSpec((256, 128), lambda i: (i, 0)),
            table,
            table,
            table,
        ],
        out_specs=(
            pl.BlockSpec((256, 128), lambda i: (i, 0)),
            pl.BlockSpec((256, QKV), lambda i: (i, 0)),
        ),
        compiler_params=pltpu.CompilerParams(vmem_limit_bytes=VMEM_LIMIT),
        cost_estimate=pl.CostEstimate(flops=4 << 30, bytes_accessed=4 << 20, transcendentals=1 << 19),
    )(at, proj, grad, *tables)


def rotary_tables(first):
    row = jnp.arange(512)
    parity, half, token = row // 256, (row // 128) % 2, row % 128
    piece = jnp.where(half == 0, first[parity], 1 - first[parity])
    position = (piece * TOK + token).astype(F32)[:, None]
    lane = jnp.arange(128) % HEAD_DIM
    halves = (lane % (ROT // 2)).astype(F32)
    frequency = jnp.power(10000.0, -2.0 * halves / ROT)[None, :]
    angle = position * frequency
    cosine, sine = jnp.cos(angle), jnp.sin(angle)
    lane = lane[None, :]
    return (
        jnp.where(lane < ROT, cosine, 1.0),
        jnp.where(lane < ROT // 2, -sine, 0.0),
        jnp.where((lane >= ROT // 2) & (lane < ROT), sine, 0.0),
    )


def gather_tokens(block):
    rel = ring_gather(block, RING_Y, 0)
    mine = jnp.concatenate([rel[0], rel[2], rel[1], rel[3]], axis=0)
    return jnp.concatenate([mine, swap_core(mine)], axis=0)


def scatter_tokens(partial):
    mine = partial[:512].astype(F32) + swap_core(partial[512:].astype(BF16)).astype(F32)
    blocks = [mine[i * TOK : (i + 1) * TOK] for i in range(4)]
    return ring_scatter([blocks[0], blocks[2], blocks[1], blocks[3]], RING_Y, 0)


def nt_dot(left, right):
    return lax.dot_general(left, right, (((1,), (1,)), ((), ())), preferred_element_type=F32)


def tn_dot(left, right):
    return lax.dot_general(left, right, (((0,), (0,)), ((), ())), preferred_element_type=F32)


def dot(left, right):
    return jnp.dot(left, right, preferred_element_type=F32)


def tail_routes():
    straight, crossed = [], []
    for s in range(2):
        for dp in range(64):
            rank, place = dp // 8, 2 * (dp % 8) + s
            target_dp = (((rank >> 1) & 1) * 16 + place) * 2 + (rank & 1)
            target = (rank >> 2) * 64 + target_dp
            straight.append((s * 64 + dp, target))
            crossed.append(((1 - s) * 64 + dp, target))
    return straight, crossed


def local(
    tokens,
    ln1_gain,
    ln1_bias,
    ln2_gain,
    ln2_bias,
    qkv_weight,
    qkv_bias,
    dense_weight,
    dense_bias,
    fc_in_weight,
    fc_in_bias,
    fc_out_weight,
    fc_out_bias,
    out_grad,
):
    s, yl, z, x, c = (lax.axis_index(a) for a in AXES)
    rank = s * 4 + yl * 2 + c
    at = jnp.stack([s, yl, z, x, c, rank]).astype(jnp.int32)
    straight, crossed = tail_routes()
    shape = jax.ShapeDtypeStruct

    small = jnp.concatenate(
        [
            jnp.stack([ln1_gain, ln1_bias, ln2_gain, ln2_bias, dense_bias, fc_out_bias], axis=1),
            qkv_bias.reshape(16, 3),
            fc_in_bias.reshape(16, 4),
        ],
        axis=1,
    )
    small = jnp.pad(small, ((0, 0), (0, 128 - small.shape[1])))
    qs_pieces, in_pieces = call(
        pack_body, (shape((4, 16, 512), BF16), shape((4, 16, 512), BF16)), (at, qkv_weight, small, fc_in_weight)
    )
    pair = ("yl", "c")
    qs = jnp.stack([qs_pieces[0]] + [exchange(qs_pieces[d], pair, 4, d) for d in range(1, 4)])
    hid = jnp.stack([in_pieces[0]] + [exchange(in_pieces[d], pair, 4, d) for d in range(1, 4)])
    tail = jnp.concatenate([dense_weight, fc_out_weight], axis=0)
    tail = lax.dynamic_slice_in_dim(tail, s * 512, 512, axis=1)
    tail = lax.ppermute(tail, AXES, straight)

    inputs = tokens.astype(F32)
    centered = inputs - jnp.mean(inputs, axis=1, keepdims=True)
    inverse = lax.rsqrt(jnp.mean(centered * centered, axis=1, keepdims=True) + EPSILON)
    normed = centered * inverse
    xh = gather_tokens(normed.astype(BF16))
    cot = gather_tokens(out_grad)

    qs = jnp.stack(ring_gather(qs, "z", 0))
    qs = call(rows_in_body, shape((WIDTH, 512), BF16), (at, *ring_gather(qs, "x", 0)))
    tail = jnp.stack(ring_gather(tail, "x", 1))
    tail = call(tail_in_body, shape((640, WIDTH), BF16), (at, *ring_gather(tail, "z", 2)))
    hid = jnp.stack(ring_gather(hid, "z", 0))
    hid = call(rows_in_body, shape((WIDTH, HID), BF16), (at, *ring_gather(hid, "x", 0)))

    w_q = qs[:, :QKV]
    params = qs[:, QKV:]
    gain_one, shift_one = params[:, 0:1].astype(F32), params[:, 1:2].astype(F32)
    gain_two, shift_two = params[:, 2:3].astype(F32), params[:, 3:4].astype(F32)
    row = jnp.arange(WIDTH)[:, None]
    column = jnp.arange(QKV)
    q_column = (column // 128) * WIDTH + rank * 128 + column % 128
    h_column = rank * HID + jnp.arange(HID)
    q_hot = (row == (q_column // 3)[None, :]).astype(BF16)
    h_hot = (row == (h_column // 4)[None, :]).astype(BF16)
    lane = jnp.arange(128)
    q_mask = lane[:, None] == (6 + q_column % 3)[None, :]
    h_mask = lane[:, None] == (9 + h_column % 4)[None, :]
    bias_q = jnp.sum(jnp.where(q_mask, tn_dot(params, q_hot), 0.0), axis=0) + tn_dot(params, w_q)[1]
    bias_h = jnp.sum(jnp.where(h_mask, tn_dot(params, h_hot), 0.0), axis=0) + tn_dot(params, hid)[3]
    scaled_q = (w_q.astype(F32) * gain_one).astype(BF16)
    scaled_h = (hid.astype(F32) * gain_two).astype(BF16)

    proj = dot(xh, scaled_q) + bias_q
    do = nt_dot(cot, tail[:128]).astype(BF16)
    y = s * 2 + yl
    first = jnp.stack([y // 2, ((y + 3) % 4) // 2])
    attended, dproj = attention(at, proj, do, rotary_tables(first))

    hidden = dot(xh, scaled_h) + bias_h
    cdf = 0.5 * (1.0 + lax.erf(hidden * (0.5**0.5)))
    active = (hidden * cdf).astype(BF16)
    slope = cdf + hidden * jnp.exp(-0.5 * hidden * hidden) * 0.3989422804014327
    dhid = (nt_dot(cot, tail[128:]) * slope).astype(BF16)

    both = jnp.concatenate([attended, active], axis=1)
    mixed_sum = scatter_tokens(dot(both, tail))
    norm_grad = scatter_tokens(nt_dot(dproj, scaled_q) + nt_dot(dhid, scaled_h))

    tail_grad = tn_dot(both, cot).astype(BF16)
    grad_q = tn_dot(xh, dproj)
    grad_h = tn_dot(xh, dhid)
    sum_q = jnp.sum(dproj.astype(F32), axis=0)
    sum_h = jnp.sum(dhid.astype(F32), axis=0)
    dw_q = gain_one * grad_q + shift_one * sum_q
    dw_h = gain_two * grad_h + shift_two * sum_h
    w_qf, w_hf = w_q.astype(F32), hid.astype(F32)
    columns = [
        jnp.sum(w_qf * grad_q, axis=1, keepdims=True),
        jnp.sum(w_qf * sum_q, axis=1, keepdims=True),
        jnp.sum(w_hf * grad_h, axis=1, keepdims=True),
        jnp.sum(w_hf * sum_h, axis=1, keepdims=True),
    ]
    ones = jnp.ones((WIDTH, 128), BF16)
    lanes = lane[None, :]
    spread_q = jnp.where(lanes == (6 + q_column % 3)[:, None], tn_dot(dproj, ones), 0.0).astype(BF16)
    spread_h = jnp.where(lanes == (9 + h_column % 4)[:, None], tn_dot(dhid, ones), 0.0).astype(BF16)
    small_grad = dot(q_hot, spread_q) + dot(h_hot, spread_h)
    bias_column = jnp.where((lanes == 4) & (rank == 0), tn_dot(cot, ones), 0.0)
    small_grad = small_grad + bias_column
    for index, value in enumerate(columns):
        small_grad = jnp.where(lanes == index, value, small_grad)
    qs_grad = jnp.concatenate([dw_q, small_grad], axis=1).astype(BF16)
    in_grad = dw_h.astype(BF16)

    piece = shape((4, 4, 16, 512), BF16)
    parts = call(rows_out_body, (piece,) * 4, (at, in_grad))
    in_sum = ring_scatter(parts, "x", 0)
    in_sum = ring_scatter([in_sum[i] for i in range(4)], "z", 0)
    piece_tail = shape((4, 80, 512), BF16)
    parts = call(tail_out_body, (piece_tail,) * 4, (at, tail_grad))
    tail_sum = ring_scatter(parts, "z", 2)
    tail_sum = ring_scatter([tail_sum[i] for i in range(4)], "x", 1).astype(BF16)
    parts = call(rows_out_body, (piece,) * 4, (at, qs_grad))
    qs_sum = ring_scatter(parts, "x", 0)
    qs_sum = ring_scatter([qs_sum[i] for i in range(4)], "z", 0)

    in_sum, qs_sum = in_sum.astype(BF16), qs_sum.astype(BF16)
    in_parts = [in_sum[0]] + [exchange(in_sum[e % 4], GROUP, 8, e) for e in range(1, 8)]
    qs_parts = [qs_sum[0]] + [exchange(qs_sum[e % 4], GROUP, 8, e) for e in range(1, 8)]
    qkv_grad, fc_in_grad, small_sum = call(
        owner_body,
        (shape((16, 3 * WIDTH), F32), shape((16, FF), F32), shape((16, 128), F32)),
        (at, *qs_parts, *in_parts),
    )
    mine = lax.ppermute(tail_sum, AXES, [(b, a) for a, b in straight])
    other = lax.ppermute(tail_sum, AXES, [(b, a) for a, b in crossed])
    is_first = s == 0
    left, right = jnp.where(is_first, mine, other), jnp.where(is_first, other, mine)
    tail_full = jnp.concatenate([left, right], axis=1).astype(F32)

    sel = jnp.where((lane == 4) | (lane == 5), 1.0, 0.0).astype(BF16)[None, :]
    out_bias = nt_dot(jnp.broadcast_to(sel, (8, 128)), params)[0:1]
    mixed = (inputs + mixed_sum + out_bias).astype(BF16)
    mean_grad = jnp.mean(norm_grad, axis=1, keepdims=True)
    mean_dot = jnp.mean(norm_grad * normed, axis=1, keepdims=True)
    tokens_grad = out_grad.astype(F32) + inverse * (norm_grad - mean_grad - normed * mean_dot)
    bias_grad = small_sum[:, 4]
    return (
        mixed,
        tokens_grad,
        small_sum[:, 0],
        small_sum[:, 1],
        small_sum[:, 2],
        small_sum[:, 3],
        qkv_grad,
        small_sum[:, 6:9].reshape(48),
        tail_full[:16],
        bias_grad,
        fc_in_grad,
        small_sum[:, 9:13].reshape(64),
        tail_full[16:],
        bias_grad,
    )


def solution(mesh):
    grid = Mesh(mesh.devices.reshape(2, 2, 4, 4, 2), AXES)
    rows = P(AXES, None)
    vector = P(AXES[1:])
    matrix = P(AXES[1:], None)
    in_specs = (
        rows,
        vector,
        vector,
        vector,
        vector,
        matrix,
        vector,
        matrix,
        vector,
        matrix,
        vector,
        matrix,
        vector,
        rows,
    )
    out_specs = (
        rows,
        rows,
        vector,
        vector,
        vector,
        vector,
        matrix,
        vector,
        matrix,
        vector,
        matrix,
        vector,
        matrix,
        vector,
    )
    return jax.shard_map(local, mesh=grid, in_specs=in_specs, out_specs=out_specs, check_vma=False)
```

```python
import jax
import jax.numpy as jnp
from jax import lax
from jax.experimental import pallas as pl
from jax.experimental.pallas import tpu as pltpu
from jax.sharding import Mesh
from jax.sharding import PartitionSpec as P

HEADS = 16
HEAD_DIM = 64
ROT = 16
WIDTH = 1024
FF = 4096
TOK = 128
F32 = jnp.float32
BF16 = jnp.bfloat16
EPSILON = 1e-05
AXES = ("s", "yl", "z", "x", "c")
GROUP = ("s", "yl", "c")
OWNERS = ("yl", "z", "x", "c")
QKV = 384
HID = 512
COLS = QKV + HID
COUNTS = (1, 1, 1, 1, 1, 1, 3, 4)
VMEM_LIMIT = 60 * 1024 * 1024


def swap_piece(values):
    return lax.ppermute(values, "s", [(0, 1), (1, 0)])


def spread(blocks, axes):
    return lax.all_to_all(blocks, axes, split_axis=0, concat_axis=0, tiled=True)


def after(values, first):
    return lax.optimization_barrier((values, first))[0]


def smem():
    return pl.BlockSpec(memory_space=pltpu.SMEM)


def vmem():
    return pl.BlockSpec(memory_space=pltpu.VMEM)


def call(body, out_shape, operands, flops=0, size=1 << 10):
    return pl.pallas_call(
        body,
        out_shape=out_shape,
        in_specs=[smem()] + [vmem()] * (len(operands) - 1),
        out_specs=jax.tree.map(lambda _: vmem(), out_shape),
        compiler_params=pltpu.CompilerParams(vmem_limit_bytes=VMEM_LIMIT),
        cost_estimate=pl.CostEstimate(flops=flops, bytes_accessed=size, transcendentals=0),
    )(*operands)


def per_owner(out, yl, c, block):
    for place in range(16):
        out[(yl * 16 + place) * 2 + c] = block


def columns_of(vector, count):
    size = 16 * count
    wide = jnp.broadcast_to(vector[...].astype(F32)[None, :], (16, size))
    row = lax.broadcasted_iota(jnp.int32, (16, size), 0)
    lane = lax.broadcasted_iota(jnp.int32, (16, size), 1)
    return [
        jnp.sum(jnp.where(lane == row * count + i, wide, 0.0), axis=1, keepdims=True) for i in range(count)
    ]


def pack_body(at, *refs):
    vectors, out, copies, done = refs[:10], refs[10], refs[11:21], refs[21]
    qkv, fc_in = copies[8:]
    started = [pltpu.make_async_copy(a, b, done.at[i]) for i, (a, b) in enumerate(zip(vectors, copies))]
    for copy in started:
        copy.start()
    for copy in started:
        copy.wait()
    lane = lax.broadcasted_iota(jnp.int32, (16, 128), 1)
    small = jnp.zeros((16, 128), F32)
    columns = []
    for vector, count in zip(copies, COUNTS):
        columns += columns_of(vector, count)
    for index, column in enumerate(columns):
        small = jnp.where(lane == index, column, small)
    small = small.astype(BF16)
    for yl in range(2):
        for c in range(2):
            parts = []
            for part in range(3):
                first = pl.multiple_of(part * WIDTH + at[0] * 512 + (yl * 2 + c) * 128, 128)
                parts.append(qkv[:, pl.ds(first, 128)])
            first = pl.multiple_of(at[0] * 2048 + (yl * 2 + c) * HID, HID)
            parts += [small, fc_in[:, pl.ds(first, HID)]]
            per_owner(out, yl, c, jnp.concatenate(parts, axis=1))


def pack(at, qkv_weight, fc_in_weight, vectors):
    anywhere = pl.BlockSpec(memory_space=pltpu.HBM)
    return pl.pallas_call(
        pack_body,
        out_shape=jax.ShapeDtypeStruct((64, 16, WIDTH), BF16),
        in_specs=[smem()] + [anywhere] * 10,
        out_specs=vmem(),
        scratch_shapes=[pltpu.VMEM((16 * count,), BF16) for count in COUNTS]
        + [pltpu.VMEM((16, 3 * WIDTH), BF16), pltpu.VMEM((16, FF), BF16), pltpu.SemaphoreType.DMA((10,))],
        compiler_params=pltpu.CompilerParams(vmem_limit_bytes=VMEM_LIMIT),
        cost_estimate=cost(0, 0),
    )(at, *vectors, qkv_weight, fc_in_weight)


def norm_stats(tokens):
    inputs = tokens[...].astype(F32)
    centered = inputs - jnp.mean(inputs, axis=1, keepdims=True)
    inverse = lax.rsqrt(jnp.mean(centered * centered, axis=1, keepdims=True) + EPSILON)
    return inputs, centered * inverse, inverse


def norm_body(at, tokens, out):
    out[...] = norm_stats(tokens)[1].astype(BF16)


def outputs_body(at, tokens, out_grad, norm_grad, mixed_sum, columns, mixed, tokens_grad):
    inputs, normed, inverse = norm_stats(tokens)
    sel = lax.broadcasted_iota(jnp.int32, (8, 128), 1)
    sel = jnp.where((sel == 4) | (sel == 5), 1.0, 0.0).astype(BF16)
    bias = nt_dot(sel, columns[:, QKV:512])[0:1]
    mixed[...] = (inputs + mixed_sum[...].astype(F32) + bias).astype(BF16)
    grad = norm_grad[...].astype(F32)
    mean_grad = jnp.mean(grad, axis=1, keepdims=True)
    mean_dot = jnp.mean(grad * normed, axis=1, keepdims=True)
    tokens_grad[...] = out_grad[...].astype(F32) + inverse * (grad - mean_grad - normed * mean_dot)


def tail_in_body(blocks, ahead, out):
    for place in range(16):
        k, lane = place // 2, (place % 2) * 512
        out[k * 16 : k * 16 + 16, lane : lane + 512] = blocks[place, 0:16, :]
        out[128 + k * 64 : 192 + k * 64, lane : lane + 512] = blocks[place, 16:80, :]


def owner_body(at, near, far, qkv_out, in_out, g1, b1, g2, b2, bias, qb, fb):
    small = jnp.zeros((16, 128), F32)
    for block, mine in ((near, at[0]), (far, 1 - at[0])):
        for j in range(4):
            for part in range(3):
                first = pl.multiple_of(part * WIDTH + mine * 512 + j * 128, 128)
                qkv_out[:, pl.ds(first, 128)] = block[j, :, part * 128 : part * 128 + 128].astype(F32)
            small = small + block[j, :, QKV:512].astype(F32)
            in_out[:, pl.ds(pl.multiple_of(mine * 2048 + j * HID, HID), HID)] = block[j, :, 512:].astype(F32)
    lane = 0
    for vector, count in ((g1, 1), (b1, 1), (g2, 1), (b2, 1), (bias, 1), (None, 1), (qb, 3), (fb, 4)):
        if vector is not None:
            size = 16 * count
            row = lax.broadcasted_iota(jnp.int32, (16, size), 0)
            place = lax.broadcasted_iota(jnp.int32, (16, size), 1)
            total = jnp.zeros((16, size), F32)
            for i in range(count):
                total = jnp.where(place == row * count + i, small[:, lane + i : lane + i + 1], total)
            vector[...] = jnp.sum(total, axis=0)
        lane += count


def nt_dot(left, right):
    return lax.dot_general(left, right, (((1,), (1,)), ((), ())), preferred_element_type=F32)


def tn_dot(left, right):
    return lax.dot_general(left, right, (((0,), (0,)), ((), ())), preferred_element_type=F32)


def dot(left, right):
    return jnp.dot(left, right, preferred_element_type=F32)


def bias_places(rank, shape, dim):
    column = lax.broadcasted_iota(jnp.int32, shape, dim)
    part, within = lax.shift_right_logical(column, 7), lax.bitwise_and(column, 127)
    q_column = part * WIDTH + rank * 128 + within
    h_column = rank * HID + column - QKV
    q_row = lax.div(q_column, 3)
    is_q = column < QKV
    row = jnp.where(is_q, q_row, lax.shift_right_logical(h_column, 2))
    lane = jnp.where(is_q, 6 + q_column - 3 * q_row, 9 + lax.bitwise_and(h_column, 3))
    return row, lane


def turn(values, cosine, low, high, sign):
    back = pltpu.roll(values, 128 - 8, 1)
    ahead = pltpu.roll(values, 8, 1)
    return values * cosine + sign * (back * low + ahead * high)


def causal():
    row = lax.broadcasted_iota(jnp.int32, (256, 256), 0)
    return row >= lax.broadcasted_iota(jnp.int32, (256, 256), 1)


def forward_body(at, xh, columns, cos, sin_low, sin_high, rotated, sums, both, slope, scaled, bias):
    rank = at[5]

    @pl.when(pl.program_id(0) == 0)
    def _():
        params = columns[:, QKV:512]
        weights = jnp.concatenate([columns[:, :QKV], columns[:, 512:]], axis=1)
        row, lane = bias_places(rank, (WIDTH, COLS), 1)
        hot = (lax.broadcasted_iota(jnp.int32, (WIDTH, COLS), 0) == row).astype(F32).astype(BF16)
        row, lane = bias_places(rank, (128, COLS), 1)
        sub = lax.broadcasted_iota(jnp.int32, (128, COLS), 0)
        column = lax.broadcasted_iota(jnp.int32, (128, COLS), 1)
        own = jnp.where(sub == lane, tn_dot(params, hot), 0.0)
        shifted = jnp.where(sub == jnp.where(column < QKV, 1, 3), tn_dot(params, weights), 0.0)
        bias[...] = jnp.sum(own + shifted, axis=0, keepdims=True)
        gains = params.astype(F32)
        scaled[:, :QKV] = (weights[:, :QKV].astype(F32) * gains[:, 0:1]).astype(BF16)
        scaled[:, QKV:] = (weights[:, QKV:].astype(F32) * gains[:, 2:3]).astype(BF16)

    tokens = xh[...].reshape(256, WIDTH)
    proj = dot(tokens, scaled[:, :QKV]) + bias[:, :QKV]
    table = cos[...], sin_low[...], sin_high[...]
    queries = turn(proj[:, 0:128], *table, 1.0).astype(BF16)
    keys = turn(proj[:, 128:256], *table, 1.0).astype(BF16)
    values = proj[:, 256:384].astype(BF16)
    rotated[...] = jnp.concatenate([queries, keys, values], axis=1).reshape(rotated.shape)
    allowed = causal()
    outs, logs = [], []
    for h in range(2):
        lanes = slice(h * HEAD_DIM, (h + 1) * HEAD_DIM)
        scores = jnp.where(allowed, nt_dot(queries[:, lanes], keys[:, lanes]) * HEAD_DIM ** (-0.5), -1e30)
        peak = jnp.max(scores, axis=1, keepdims=True)
        weights = jnp.exp(scores - peak)
        norm = jnp.sum(weights, axis=1, keepdims=True)
        outs.append(dot((weights / norm).astype(BF16), values[:, lanes]))
        logs.append(jnp.broadcast_to(peak + jnp.log(norm), (256, HEAD_DIM)))
    sums[...] = jnp.concatenate(logs, axis=1).reshape(sums.shape)
    attended = jnp.concatenate(outs, axis=1).astype(BF16)
    hidden = dot(tokens, scaled[:, QKV:]) + bias[:, QKV:]
    cdf = 0.5 * (1.0 + lax.erf(hidden * (0.5**0.5)))
    both[...] = jnp.concatenate([attended, (hidden * cdf).astype(BF16)], axis=1).reshape(both.shape)
    slope[...] = (cdf + hidden * jnp.exp(-0.5 * hidden * hidden) * 0.3989422804014327).reshape(slope.shape)


def token_spec(lanes):
    return pl.BlockSpec((2, 1, TOK, lanes), lambda i: (0, i, 0, 0))


def token_shape(lanes, dtype):
    return jax.ShapeDtypeStruct((2, 4, TOK, lanes), dtype)


def whole(rows, lanes):
    return pl.BlockSpec((rows, lanes), lambda i: (0, 0))


def cost(flops, size):
    return pl.CostEstimate(flops=flops >> 10, bytes_accessed=size >> 10, transcendentals=0)


def forward(at, xh, columns, tables):
    table = whole(256, 128)
    return pl.pallas_call(
        forward_body,
        grid=(4,),
        out_shape=(
            token_shape(QKV, BF16),
            token_shape(128, F32),
            token_shape(128 + HID, BF16),
            token_shape(HID, F32),
            jax.ShapeDtypeStruct((WIDTH, COLS), BF16),
        ),
        in_specs=[smem(), token_spec(WIDTH), whole(WIDTH, WIDTH), table, table, table],
        out_specs=(
            token_spec(QKV),
            token_spec(128),
            token_spec(128 + HID),
            token_spec(HID),
            whole(WIDTH, COLS),
        ),
        scratch_shapes=[pltpu.VMEM((1, COLS), F32)],
        compiler_params=pltpu.CompilerParams(vmem_limit_bytes=VMEM_LIMIT),
        cost_estimate=cost(4 << 30, 8 << 20),
    )(at, xh, columns, *tables)


def mixed_body(both, tail, out):
    features = both[...].reshape(256, 128 + HID)
    out[...] = dot(features, tail[...]).astype(BF16).reshape(out.shape)


def mixed_of(both, tail):
    return pl.pallas_call(
        mixed_body,
        grid=(4,),
        out_shape=token_shape(WIDTH, BF16),
        in_specs=[token_spec(128 + HID), whole(640, WIDTH)],
        out_specs=token_spec(WIDTH),
        compiler_params=pltpu.CompilerParams(vmem_limit_bytes=VMEM_LIMIT),
        cost_estimate=cost(2 << 30, 6 << 20),
    )(both, tail)


def sequence_step(rotated, sums, slope, cot, tail, scaled, cos, sin_low, sin_high, grads, norm):
    cotangent = cot[...].reshape(256, WIDTH)
    table = cos[...], sin_low[...], sin_high[...]
    packed, logs = rotated[...].reshape(256, QKV), sums[...].reshape(256, 128)
    grad = nt_dot(cotangent, tail[:128]).astype(BF16)
    dhid = (nt_dot(cotangent, tail[128:]) * slope[...].reshape(256, HID)).astype(BF16)
    allowed = causal()
    dqs, dks, dvs = [], [], []
    scale = HEAD_DIM ** (-0.5)
    for h in range(2):
        q, k, v = (packed[:, i * 128 + h * HEAD_DIM : i * 128 + (h + 1) * HEAD_DIM] for i in range(3))
        g = grad[:, h * HEAD_DIM : (h + 1) * HEAD_DIM]
        scores = nt_dot(q, k) * scale - logs[:, h * HEAD_DIM : h * HEAD_DIM + 1]
        probs = jnp.exp(jnp.where(allowed, scores, -1e30))
        dprobs = nt_dot(g, v)
        inner = jnp.sum(probs * dprobs, axis=1, keepdims=True)
        ds = (probs * (dprobs - inner)).astype(BF16)
        dqs.append(dot(ds, k) * scale)
        dks.append(tn_dot(ds, q) * scale)
        dvs.append(tn_dot(probs.astype(BF16), g))
    dq = turn(jnp.concatenate(dqs, axis=1).astype(BF16).astype(F32), *table, -1.0)
    dk = turn(jnp.concatenate(dks, axis=1).astype(BF16).astype(F32), *table, -1.0)
    dv = jnp.concatenate(dvs, axis=1)
    back = jnp.concatenate([dq.astype(BF16), dk.astype(BF16), dv.astype(BF16), dhid], axis=1)
    grads[:, pl.program_id(0)] = back.reshape(2, TOK, COLS)
    norm[...] = nt_dot(back, scaled[...]).astype(BF16).reshape(norm.shape)


def columns_step(at, xh, columns, total, out, stored, sums, spots):
    rank, block = at[5], pl.program_id(0) - 4
    grads = stored[...].reshape(WIDTH, COLS)

    @pl.when(block == 0)
    def _():
        sums[...] = dot(jnp.ones((8, WIDTH), BF16), grads)
        row, lane = bias_places(rank, (128, COLS), 1)
        sub = lax.broadcasted_iota(jnp.int32, (128, COLS), 0)
        spots[...] = jnp.where(sub == lane, sums[0:1, :], 0.0).astype(BF16)

    product = tn_dot(xh[...], grads)
    total_cols = sums[0:1, :]
    params = columns[:, QKV:512].astype(F32)
    weights = jnp.concatenate([columns[:, :QKV], columns[:, 512:]], axis=1).astype(F32)
    row, lane = bias_places(rank, (256, COLS), 1)
    here = block * 256 + lax.broadcasted_iota(jnp.int32, (256, COLS), 0)
    hot = (here == row).astype(F32).astype(BF16)
    small = nt_dot(hot, spots[...])
    lane = lax.broadcasted_iota(jnp.int32, (256, 128), 1)
    mirror = lax.broadcasted_iota(jnp.int32, (256, 256), 0) == lax.broadcasted_iota(jnp.int32, (256, 256), 1)
    mine = jnp.sum(jnp.where(mirror, total[0:1, :], 0.0), axis=1, keepdims=True)
    small = jnp.where((lane == 4) & (rank == 0), mine, small)
    for first, last, index in ((0, QKV, 0), (QKV, COLS, 2)):
        w, g, t = weights[:, first:last], product[:, first:last], total_cols[:, first:last]
        small = jnp.where(lane == index, jnp.sum(w * g, axis=1, keepdims=True), small)
        small = jnp.where(lane == index + 1, jnp.sum(w * t, axis=1, keepdims=True), small)
        change = (params[:, index : index + 1] * g + params[:, index + 1 : index + 2] * t).astype(BF16)
        start = 0 if first == 0 else 512
        out[:, start : start + last - first] = change
    out[:, QKV:512] = small.astype(BF16)


def backward_body(
    at, rotated, sums, slope, cot, tail, scaled, cos, sin_low, sin_high, xh, columns, total, one, two, norm, out, grads, cols, spots
):
    @pl.when(pl.program_id(0) < 4)
    def _():
        sequence_step(rotated, sums, slope, cot, tail, scaled, cos, sin_low, sin_high, grads, norm)

    @pl.when(pl.program_id(0) >= 4)
    def _():
        columns_step(at, xh, columns, total, out, grads, cols, spots)


def backward(at, rotated, sums, slope, cot, tail, scaled, tables, xh, columns, total, one, two):
    def tokens(lanes):
        return pl.BlockSpec((2, 1, TOK, lanes), lambda i: (0, jnp.minimum(i, 3), 0, 0))

    def later(i):
        return jnp.maximum(i - 4, 0)

    table = whole(256, 128)
    anywhere = pl.BlockSpec(memory_space=pl.ANY)
    return pl.pallas_call(
        backward_body,
        grid=(8,),
        out_shape=(token_shape(WIDTH, BF16), jax.ShapeDtypeStruct((WIDTH, WIDTH), BF16)),
        in_specs=[
            smem(),
            tokens(QKV),
            tokens(128),
            tokens(HID),
            tokens(WIDTH),
            whole(640, WIDTH),
            whole(WIDTH, COLS),
            table,
            table,
            table,
            pl.BlockSpec((WIDTH, 256), lambda i: (0, later(i))),
            pl.BlockSpec((256, WIDTH), lambda i: (later(i), 0)),
            pl.BlockSpec((8, 256), lambda i: (0, later(i))),
            anywhere,
            anywhere,
        ],
        out_specs=(tokens(WIDTH), pl.BlockSpec((256, WIDTH), lambda i: (later(i), 0))),
        scratch_shapes=[
            pltpu.VMEM((2, 4, TOK, COLS), BF16),
            pltpu.VMEM((8, COLS), F32),
            pltpu.VMEM((128, COLS), BF16),
        ],
        compiler_params=pltpu.CompilerParams(vmem_limit_bytes=VMEM_LIMIT),
        cost_estimate=cost(6 << 30, 16 << 20),
    )(at, rotated, sums, slope, cot, tail, scaled, *tables, xh, columns, total, one, two)


def tail_grad_body(both, cot, out, total):
    for half in range(2):
        product = tn_dot(both[...], cot[:, half * 512 : half * 512 + 512]).astype(BF16)
        for k in range(8):
            out[2 * k + half, 0:16, :] = product[k * 16 : k * 16 + 16]
            out[2 * k + half, 16:80, :] = product[128 + k * 64 : 192 + k * 64]
    total[...] = dot(jnp.ones((8, WIDTH), BF16), cot[...])


def tail_grad_of(both, cot):
    return pl.pallas_call(
        tail_grad_body,
        out_shape=(jax.ShapeDtypeStruct((16, 80, 512), BF16), jax.ShapeDtypeStruct((8, WIDTH), F32)),
        in_specs=[vmem(), vmem()],
        out_specs=(vmem(), vmem()),
        compiler_params=pltpu.CompilerParams(vmem_limit_bytes=VMEM_LIMIT),
        cost_estimate=cost(2 << 30, 6 << 20),
    )(both, cot)


def tail_in(blocks, ahead):
    return pl.pallas_call(
        tail_in_body,
        out_shape=jax.ShapeDtypeStruct((640, WIDTH), BF16),
        in_specs=[vmem(), pl.BlockSpec(memory_space=pl.ANY)],
        out_specs=vmem(),
        compiler_params=pltpu.CompilerParams(vmem_limit_bytes=VMEM_LIMIT),
        cost_estimate=cost(0, 0),
    )(blocks, ahead)


def rotary_tables():
    position = jnp.arange(256).astype(F32)[:, None]
    lane = jnp.arange(128) % HEAD_DIM
    halves = (lane % (ROT // 2)).astype(F32)
    frequency = jnp.power(10000.0, -2.0 * halves / ROT)[None, :]
    angle = position * frequency
    cosine, sine = jnp.cos(angle), jnp.sin(angle)
    lane = lane[None, :]
    return (
        jnp.where(lane < ROT, cosine, 1.0),
        jnp.where(lane < ROT // 2, -sine, 0.0),
        jnp.where((lane >= ROT // 2) & (lane < ROT), sine, 0.0),
    )


def gather_tokens(block):
    return lax.all_gather(block, GROUP, axis=0, tiled=True)


def scatter_tokens(partial):
    return lax.psum_scatter(partial, GROUP, scatter_dimension=0, tiled=True)


def tail_routes():
    straight, crossed = [], []
    for s in range(2):
        for dp in range(64):
            rank, place = dp // 8, 2 * (dp % 8) + s
            target_dp = (((rank >> 1) & 1) * 16 + place) * 2 + (rank & 1)
            target = (rank >> 2) * 64 + target_dp
            straight.append((s * 64 + dp, target))
            crossed.append(((1 - s) * 64 + dp, target))
    return straight, crossed


def local(
    tokens,
    ln1_gain,
    ln1_bias,
    ln2_gain,
    ln2_bias,
    qkv_weight,
    qkv_bias,
    dense_weight,
    dense_bias,
    fc_in_weight,
    fc_in_bias,
    fc_out_weight,
    fc_out_bias,
    out_grad,
):
    s, yl, z, x, c = (lax.axis_index(a) for a in AXES)
    rank = s * 4 + yl * 2 + c
    at = jnp.stack([s, yl, z, x, c, rank]).astype(jnp.int32)
    straight, crossed = tail_routes()
    shape = jax.ShapeDtypeStruct

    vectors = (ln1_gain, ln1_bias, ln2_gain, ln2_bias, dense_bias, fc_out_bias, qkv_bias, fc_in_bias)
    sent = pack(at, qkv_weight, fc_in_weight, vectors)
    columns_in = spread(sent, OWNERS).reshape(WIDTH, 1024)
    tail = jnp.concatenate([dense_weight, fc_out_weight], axis=0)
    tail = lax.dynamic_slice_in_dim(tail, s * 512, 512, axis=1)
    tail = lax.ppermute(tail, AXES, straight)
    tail = spread(jnp.broadcast_to(after(tail, columns_in), (16, 80, 512)), ("z", "x"))

    own_xh = call(norm_body, shape((TOK, WIDTH), BF16), (at, tokens))
    xh = gather_tokens(own_xh)
    cot = gather_tokens(after(out_grad, own_xh))

    xh_tokens, cot_tokens = xh.reshape(2, 4, TOK, WIDTH), cot.reshape(2, 4, TOK, WIDTH)
    tables = rotary_tables()
    rotated, sums, both, slope, scaled = forward(at, xh_tokens, columns_in, tables)
    tail = tail_in(tail, slope)
    tail_grad, total = tail_grad_of(both.reshape(WIDTH, 640), cot)
    tail_parts = spread(tail_grad, ("z", "x"))
    mixed_part = mixed_of(both, tail)
    mixed_sum = scatter_tokens(mixed_part.reshape(WIDTH, WIDTH))
    norm_part, columns_grad = backward(
        at, rotated, sums, slope, cot_tokens, tail, scaled, tables, xh, columns_in, total, tail_grad, mixed_part
    )
    norm_part, columns_grad = after((norm_part, columns_grad), (mixed_sum, tail_parts))
    norm_grad = scatter_tokens(norm_part.reshape(WIDTH, WIDTH))
    tail_sum = jnp.sum(tail_parts.astype(F32), axis=0).astype(BF16)
    parts = spread(columns_grad.reshape(64, 16, 1024), OWNERS).reshape(2, 16, 2, 16, 1024)
    near = jnp.sum(parts.astype(F32), axis=1).reshape(4, 16, 1024)
    far = swap_piece(near.astype(BF16))
    vector = shape((16,), F32)
    qkv_grad, fc_in_grad, g1_grad, b1_grad, g2_grad, b2_grad, bias_grad, qb_grad, fb_grad = call(
        owner_body,
        (shape((16, 3 * WIDTH), F32), shape((16, FF), F32))
        + (vector,) * 5
        + (shape((48,), F32), shape((64,), F32)),
        (at, near, far),
    )
    mine = lax.ppermute(tail_sum, AXES, [(b, a) for a, b in straight])
    other = lax.ppermute(tail_sum, AXES, [(b, a) for a, b in crossed])
    is_first = s == 0
    left, right = jnp.where(is_first, mine, other), jnp.where(is_first, other, mine)
    tail_full = jnp.concatenate([left, right], axis=1).astype(F32)

    mixed, tokens_grad = call(
        outputs_body,
        (shape((TOK, WIDTH), BF16), shape((TOK, WIDTH), F32)),
        (at, tokens, out_grad, norm_grad, mixed_sum, columns_in),
    )
    return (
        mixed,
        tokens_grad,
        g1_grad,
        b1_grad,
        g2_grad,
        b2_grad,
        qkv_grad,
        qb_grad,
        tail_full[:16],
        bias_grad,
        fc_in_grad,
        fb_grad,
        tail_full[16:],
        bias_grad,
    )


def solution(mesh):
    grid = Mesh(mesh.devices.reshape(2, 2, 4, 4, 2), AXES)
    rows = P(AXES, None)
    vector = P(AXES[1:])
    matrix = P(AXES[1:], None)
    in_specs = (
        rows,
        vector,
        vector,
        vector,
        vector,
        matrix,
        vector,
        matrix,
        vector,
        matrix,
        vector,
        matrix,
        vector,
        rows,
    )
    out_specs = (
        rows,
        rows,
        vector,
        vector,
        vector,
        vector,
        matrix,
        vector,
        matrix,
        vector,
        matrix,
        vector,
        matrix,
        vector,
    )
    return jax.shard_map(local, mesh=grid, in_specs=in_specs, out_specs=out_specs, check_vma=False)
```

```python
import jax
import jax.numpy as jnp
from jax import lax
from jax.experimental import pallas as pl
from jax.experimental.pallas import tpu as pltpu
from jax.sharding import Mesh
from jax.sharding import PartitionSpec as P

HEADS = 16
HEAD_DIM = 64
ROT = 16
WIDTH = 1024
FF = 4096
TOK = 128
F32 = jnp.float32
BF16 = jnp.bfloat16
EPSILON = 1e-05
AXES = ("s", "yl", "z", "x", "c")
GROUP = ("s", "yl", "c")
PAIR = ("yl", "c")
PLACES = ("z", "x")
QKV = 384
HID = 512
COLS = QKV + HID
COUNTS = (1, 1, 1, 1, 1, 1, 3, 4)
VMEM_LIMIT = 60 * 1024 * 1024


def exchange(values, axes, count, mask):
    return lax.ppermute(values, axes, [(i, i ^ mask) for i in range(count)])


def spread(blocks, axes):
    return lax.all_to_all(blocks, axes, split_axis=0, concat_axis=0, tiled=True)


def after(values, first):
    return lax.optimization_barrier((values, first))[0]


def smem():
    return pl.BlockSpec(memory_space=pltpu.SMEM)


def vmem():
    return pl.BlockSpec(memory_space=pltpu.VMEM)


def call(body, out_shape, operands, ordered=False):
    return pl.pallas_call(
        body,
        out_shape=out_shape,
        in_specs=[smem()] + [vmem()] * (len(operands) - 1 - ordered) + [pl.BlockSpec(memory_space=pl.ANY)] * ordered,
        out_specs=jax.tree.map(lambda _: vmem(), out_shape),
        compiler_params=pltpu.CompilerParams(vmem_limit_bytes=VMEM_LIMIT),
        cost_estimate=pl.CostEstimate(flops=0, bytes_accessed=1 << 10, transcendentals=0),
    )(*operands)


def columns_of(vector, count):
    size = 16 * count
    wide = jnp.broadcast_to(vector[...].astype(F32)[None, :], (16, size))
    row = lax.broadcasted_iota(jnp.int32, (16, size), 0)
    lane = lax.broadcasted_iota(jnp.int32, (16, size), 1)
    return [
        jnp.sum(jnp.where(lane == row * count + i, wide, 0.0), axis=1, keepdims=True) for i in range(count)
    ]


def pack_body(at, *refs):
    vectors, out, copies, done = refs[:10], refs[10], refs[11:21], refs[21]
    qkv, fc_in = copies[8:]
    started = [pltpu.make_async_copy(a, b, done.at[i]) for i, (a, b) in enumerate(zip(vectors, copies))]
    for copy in started:
        copy.start()
    for copy in started:
        copy.wait()
    lane = lax.broadcasted_iota(jnp.int32, (16, 128), 1)
    small = jnp.zeros((16, 128), F32)
    columns = []
    for vector, count in zip(copies, COUNTS):
        columns += columns_of(vector, count)
    for index, column in enumerate(columns):
        small = jnp.where(lane == index, column, small)
    small = small.astype(BF16)
    for d in range(4):
        rank = lax.bitwise_xor(at[5], d)
        parts = []
        for part in range(3):
            first = pl.multiple_of(part * WIDTH + rank * 128, 128)
            parts.append(qkv[:, pl.ds(first, 128)])
        parts += [small, fc_in[:, pl.ds(pl.multiple_of(rank * HID, HID), HID)]]
        out[d] = jnp.concatenate(parts, axis=1)


def pack(at, qkv_weight, fc_in_weight, vectors):
    anywhere = pl.BlockSpec(memory_space=pltpu.HBM)
    return pl.pallas_call(
        pack_body,
        out_shape=jax.ShapeDtypeStruct((4, 16, WIDTH), BF16),
        in_specs=[smem()] + [anywhere] * 10,
        out_specs=vmem(),
        scratch_shapes=[pltpu.VMEM((16 * count,), BF16) for count in COUNTS]
        + [pltpu.VMEM((16, 3 * WIDTH), BF16), pltpu.VMEM((16, FF), BF16), pltpu.SemaphoreType.DMA((10,))],
        compiler_params=pltpu.CompilerParams(vmem_limit_bytes=VMEM_LIMIT),
        cost_estimate=cost(0, 0),
    )(at, *vectors, qkv_weight, fc_in_weight)


def norm_stats(tokens):
    inputs = tokens[...].astype(F32)
    centered = inputs - jnp.mean(inputs, axis=1, keepdims=True)
    inverse = lax.rsqrt(jnp.mean(centered * centered, axis=1, keepdims=True) + EPSILON)
    return inputs, centered * inverse, inverse


def norm_body(at, tokens, ahead, out):
    out[...] = norm_stats(tokens)[1].astype(BF16)


def outputs_body(at, tokens, out_grad, norm_grad, mixed_sum, columns, mixed, tokens_grad):
    inputs, normed, inverse = norm_stats(tokens)
    sel = lax.broadcasted_iota(jnp.int32, (8, 128), 1)
    sel = jnp.where((sel == 4) | (sel == 5), 1.0, 0.0).astype(BF16)
    bias = nt_dot(sel, columns[:, QKV:512])[0:1]
    mixed[...] = (inputs + mixed_sum[...].astype(F32) + bias).astype(BF16)
    grad = norm_grad[...].astype(F32)
    mean_grad = jnp.mean(grad, axis=1, keepdims=True)
    mean_dot = jnp.mean(grad * normed, axis=1, keepdims=True)
    tokens_grad[...] = out_grad[...].astype(F32) + inverse * (grad - mean_grad - normed * mean_dot)


def owner_body(at, *refs):
    pieces, mine, other, ahead = refs[:4]
    (qkv_out, in_out, g1, b1, g2, b2, bias, same, qb, fb, dense_out, fc_out) = refs[4:]
    for half, part in ((at[0], mine), (1 - at[0], other)):
        lanes = pl.ds(pl.multiple_of(half * 512, 512), 512)
        dense_out[:, lanes] = part[0:16].astype(F32)
        fc_out[:, lanes] = part[16:80].astype(F32)
    small = jnp.zeros((16, 128), F32)
    for rank in range(8):
        block = pieces[rank]
        for part in range(3):
            first = part * WIDTH + rank * 128
            qkv_out[:, first : first + 128] = block[:, part * 128 : part * 128 + 128].astype(F32)
        small = small + block[:, QKV:512].astype(F32)
        in_out[:, rank * HID : rank * HID + HID] = block[:, 512:].astype(F32)
    lane = 0
    for vector, count in ((g1, 1), (b1, 1), (g2, 1), (b2, 1), (bias, 1), (None, 1), (qb, 3), (fb, 4)):
        if vector is not None:
            size = 16 * count
            row = lax.broadcasted_iota(jnp.int32, (16, size), 0)
            place = lax.broadcasted_iota(jnp.int32, (16, size), 1)
            total = jnp.zeros((16, size), F32)
            for i in range(count):
                total = jnp.where(place == row * count + i, small[:, lane + i : lane + i + 1], total)
            vector[...] = jnp.sum(total, axis=0)
            if vector is bias:
                same[...] = jnp.sum(total, axis=0)
        lane += count


def nt_dot(left, right):
    return lax.dot_general(left, right, (((1,), (1,)), ((), ())), preferred_element_type=F32)


def tn_dot(left, right):
    return lax.dot_general(left, right, (((0,), (0,)), ((), ())), preferred_element_type=F32)


def dot(left, right):
    return jnp.dot(left, right, preferred_element_type=F32)


def bias_places(rank, shape, dim):
    column = lax.broadcasted_iota(jnp.int32, shape, dim)
    part, within = lax.shift_right_logical(column, 7), lax.bitwise_and(column, 127)
    q_column = part * WIDTH + rank * 128 + within
    h_column = rank * HID + column - QKV
    q_row = lax.div(q_column, 3)
    is_q = column < QKV
    row = jnp.where(is_q, q_row, lax.shift_right_logical(h_column, 2))
    lane = jnp.where(is_q, 6 + q_column - 3 * q_row, 9 + lax.bitwise_and(h_column, 3))
    return row, lane


def turn(values, cosine, low, high, sign):
    back = pltpu.roll(values, 128 - 8, 1)
    ahead = pltpu.roll(values, 8, 1)
    return values * cosine + sign * (back * low + ahead * high)


def causal():
    row = lax.broadcasted_iota(jnp.int32, (256, 256), 0)
    return row >= lax.broadcasted_iota(jnp.int32, (256, 256), 1)


def owner_rows(at, place, d):
    pair = lax.bitwise_xor(at[1] * 2 + at[4], d)
    return pl.multiple_of((lax.shift_right_logical(pair, 1) * 16 + place) * 32 + lax.bitwise_and(pair, 1) * 16, 16)


def forward_body(at, xh, pieces, cos, sin_low, sin_high, rotated, sums, both, slope, turned, columns, hot, flipped, scaled, bias):
    rank = at[5]

    @pl.when(pl.program_id(0) == 0)
    def _():
        for place in range(16):
            for d in range(4):
                columns[pl.ds(owner_rows(at, place, d), 16), :] = pieces[place, d]
        params = columns[:, QKV:512]
        weights = jnp.concatenate([columns[:, :QKV], columns[:, 512:]], axis=1)
        row, lane = bias_places(rank, (WIDTH, COLS), 1)
        hot[...] = (lax.broadcasted_iota(jnp.int32, (WIDTH, COLS), 0) == row).astype(F32).astype(BF16)
        row, lane = bias_places(rank, (128, COLS), 1)
        sub = lax.broadcasted_iota(jnp.int32, (128, COLS), 0)
        column = lax.broadcasted_iota(jnp.int32, (128, COLS), 1)
        own = jnp.where(sub == lane, tn_dot(params, hot[...]), 0.0)
        shifted = jnp.where(sub == jnp.where(column < QKV, 1, 3), tn_dot(params, weights), 0.0)
        bias[...] = jnp.sum(own + shifted, axis=0, keepdims=True)
        gains = params.astype(F32)
        scaled[:, :QKV] = (weights[:, :QKV].astype(F32) * gains[:, 0:1]).astype(BF16)
        scaled[:, QKV:] = (weights[:, QKV:].astype(F32) * gains[:, 2:3]).astype(BF16)
        turned[...] = scaled[...].T

    tokens = xh[...].reshape(256, WIDTH)
    for piece in range(2):
        first = pl.multiple_of(piece * 512 + pl.program_id(0) * TOK, TOK)
        flipped[:, pl.ds(first, TOK)] = tokens[piece * TOK : piece * TOK + TOK].T
    proj = dot(tokens, scaled[:, :QKV]) + bias[:, :QKV]
    table = cos[...], sin_low[...], sin_high[...]
    queries = turn(proj[:, 0:128], *table, 1.0).astype(BF16)
    keys = turn(proj[:, 128:256], *table, 1.0).astype(BF16)
    values = proj[:, 256:384].astype(BF16)
    rotated[...] = jnp.concatenate([queries, keys, values], axis=1).reshape(rotated.shape)
    allowed = causal()
    outs, logs = [], []
    for h in range(2):
        lanes = slice(h * HEAD_DIM, (h + 1) * HEAD_DIM)
        scores = jnp.where(allowed, nt_dot(queries[:, lanes], keys[:, lanes]) * HEAD_DIM ** (-0.5), -1e30)
        peak = jnp.max(scores, axis=1, keepdims=True)
        weights = jnp.exp(scores - peak)
        norm = jnp.sum(weights, axis=1, keepdims=True)
        outs.append(dot((weights / norm).astype(BF16), values[:, lanes]))
        logs.append(jnp.broadcast_to(peak + jnp.log(norm), (256, HEAD_DIM)))
    sums[...] = jnp.concatenate(logs, axis=1).reshape(sums.shape)
    attended = jnp.concatenate(outs, axis=1).astype(BF16)
    hidden = dot(tokens, scaled[:, QKV:]) + bias[:, QKV:]
    cdf = 0.5 * (1.0 + lax.erf(hidden * (0.5**0.5)))
    both[...] = jnp.concatenate([attended, (hidden * cdf).astype(BF16)], axis=1).reshape(both.shape)
    slope[...] = (cdf + hidden * jnp.exp(-0.5 * hidden * hidden) * 0.3989422804014327).astype(BF16).reshape(slope.shape)


def token_spec(lanes):
    return pl.BlockSpec((2, 1, TOK, lanes), lambda i: (0, i, 0, 0))


def token_shape(lanes, dtype):
    return jax.ShapeDtypeStruct((2, 4, TOK, lanes), dtype)


def whole(rows, lanes):
    return pl.BlockSpec((rows, lanes), lambda i: (0, 0))


def cost(flops, size):
    return pl.CostEstimate(flops=flops >> 10, bytes_accessed=size >> 10, transcendentals=0)


def forward(at, xh, pieces, tables):
    table = whole(256, 128)
    return pl.pallas_call(
        forward_body,
        grid=(4,),
        out_shape=(
            token_shape(QKV, BF16),
            token_shape(128, F32),
            token_shape(128 + HID, BF16),
            token_shape(HID, BF16),
            jax.ShapeDtypeStruct((COLS, WIDTH), BF16),
            jax.ShapeDtypeStruct((WIDTH, WIDTH), BF16),
            jax.ShapeDtypeStruct((WIDTH, COLS), BF16),
            jax.ShapeDtypeStruct((WIDTH, WIDTH), BF16),
        ),
        in_specs=[
            smem(),
            token_spec(WIDTH),
            pl.BlockSpec((16, 4, 16, WIDTH), lambda i: (0, 0, 0, 0)),
            table,
            table,
            table,
        ],
        out_specs=(
            token_spec(QKV),
            token_spec(128),
            token_spec(128 + HID),
            token_spec(HID),
            whole(COLS, WIDTH),
            whole(WIDTH, WIDTH),
            whole(WIDTH, COLS),
            whole(WIDTH, WIDTH),
        ),
        scratch_shapes=[pltpu.VMEM((WIDTH, COLS), BF16), pltpu.VMEM((1, COLS), F32)],
        compiler_params=pltpu.CompilerParams(vmem_limit_bytes=VMEM_LIMIT),
        cost_estimate=cost(4 << 30, 8 << 20),
    )(at, xh, pieces, *tables)


def mixed_body(both, blocks, ahead, out_ref, turned, both_here, blocks_here, tail, buffer, done, written):
    started = fetch((blocks, both), (blocks_here, both_here), done)
    started[0].wait()
    for place in range(16):
        k, lane = place // 2, (place % 2) * 512
        tail[k * 16 : k * 16 + 16, lane : lane + 512] = blocks_here[place, 0:16, :]
        tail[128 + k * 64 : 192 + k * 64, lane : lane + 512] = blocks_here[place, 16:80, :]
    started[1].wait()
    stores = []
    for i in range(4):
        product = dot(both_here[:, i].reshape(256, 128 + HID), tail[...])
        buffer[:, i] = product.astype(BF16).reshape(2, TOK, WIDTH)
        stores.append(pltpu.make_async_copy(buffer.at[:, i], out_ref.at[:, i], written.at[i]))
        stores[-1].start()
    turned[...] = tail[...].T
    for copy in stores:
        copy.wait()


def mixed_of(both, blocks, ahead):
    remote = pl.BlockSpec(memory_space=pltpu.HBM)
    return pl.pallas_call(
        mixed_body,
        out_shape=(token_shape(WIDTH, BF16), jax.ShapeDtypeStruct((WIDTH, 640), BF16)),
        in_specs=[remote, remote, pl.BlockSpec(memory_space=pl.ANY)],
        out_specs=(remote, vmem()),
        scratch_shapes=[
            pltpu.VMEM(both.shape, BF16),
            pltpu.VMEM(blocks.shape, BF16),
            pltpu.VMEM((640, WIDTH), BF16),
            pltpu.VMEM((2, 4, TOK, WIDTH), BF16),
            pltpu.SemaphoreType.DMA((2,)),
            pltpu.SemaphoreType.DMA((4,)),
        ],
        compiler_params=pltpu.CompilerParams(vmem_limit_bytes=VMEM_LIMIT),
        cost_estimate=cost(2 << 30, 6 << 20),
    )(both, blocks, ahead)


def sequence_step(packed, logs, slope, cotangent, tail, table):
    grad = dot(cotangent, tail[:, :128]).astype(BF16)
    dhid = (dot(cotangent, tail[:, 128:]) * slope.astype(F32)).astype(BF16)
    allowed = causal()
    dqs, dks, dvs = [], [], []
    scale = HEAD_DIM ** (-0.5)
    for h in range(2):
        q, k, v = (packed[:, i * 128 + h * HEAD_DIM : i * 128 + (h + 1) * HEAD_DIM] for i in range(3))
        g = grad[:, h * HEAD_DIM : (h + 1) * HEAD_DIM]
        scores = nt_dot(q, k) * scale - logs[:, h * HEAD_DIM : h * HEAD_DIM + 1]
        probs = jnp.exp(jnp.where(allowed, scores, -1e30))
        dprobs = nt_dot(g, v)
        inner = jnp.sum(probs * dprobs, axis=1, keepdims=True)
        ds = (probs * (dprobs - inner)).astype(BF16)
        dqs.append(dot(ds, k) * scale)
        dks.append(tn_dot(ds, q) * scale)
        dvs.append(tn_dot(probs.astype(BF16), g))
    dq = turn(jnp.concatenate(dqs, axis=1).astype(BF16).astype(F32), *table, -1.0)
    dk = turn(jnp.concatenate(dks, axis=1).astype(BF16).astype(F32), *table, -1.0)
    dv = jnp.concatenate(dvs, axis=1)
    back = jnp.concatenate([dq.astype(BF16), dk.astype(BF16), dv.astype(BF16), dhid], axis=1)
    return back


def columns_step(rank, block, xh, columns, hot, total, grads, total_cols, spots):
    product = dot(xh, grads)
    params = columns[:, QKV:512].astype(F32)
    weights = jnp.concatenate([columns[:, :QKV], columns[:, 512:]], axis=1).astype(F32)
    small = nt_dot(hot, spots)
    lane = lax.broadcasted_iota(jnp.int32, (256, 128), 1)
    mirror = lax.broadcasted_iota(jnp.int32, (256, 256), 0) == lax.broadcasted_iota(jnp.int32, (256, 256), 1)
    mine = jnp.sum(jnp.where(mirror, total, 0.0), axis=1, keepdims=True)
    small = jnp.where((lane == 4) & (rank == 0), mine, small)
    changes = []
    for first, last, index in ((0, QKV, 0), (QKV, COLS, 2)):
        w, g, t = weights[:, first:last], product[:, first:last], total_cols[:, first:last]
        small = jnp.where(lane == index, jnp.sum(w * g, axis=1, keepdims=True), small)
        small = jnp.where(lane == index + 1, jnp.sum(w * t, axis=1, keepdims=True), small)
        change = (params[:, index : index + 1] * g + params[:, index + 1 : index + 2] * t).astype(BF16)
        changes.append(change)
    return jnp.concatenate([changes[0], small.astype(BF16), changes[1]], axis=1)


def fetch(sources, copies, done):
    started = [pltpu.make_async_copy(a, b, done.at[i]) for i, (a, b) in enumerate(zip(sources, copies))]
    for copy in started:
        copy.start()
    return started


def backward_body(at, *refs):
    sources, (norm_out, columns_out), copies = refs[:13], refs[15:17], refs[17:30]
    grads, norm_buffer, columns_buffer, done, written = refs[30:]
    cot, tail, rotated, sums, slope, cos, sin_low, sin_high, scaled, total, xh, columns, hot = copies
    started = fetch(sources, copies, done)
    for copy in started[:8]:
        copy.wait()
    table = cos[...], sin_low[...], sin_high[...]
    stores = []
    for i in range(4):
        back = sequence_step(
            rotated[:, i].reshape(256, QKV),
            sums[:, i].reshape(256, 128),
            slope[:, i].reshape(256, HID),
            cot[:, i].reshape(256, WIDTH),
            tail,
            table,
        )
        grads[:, i] = back.reshape(2, TOK, COLS)
        if i == 0:
            started[8].wait()
        norm_buffer[:, i] = dot(back, scaled[...]).astype(BF16).reshape(2, TOK, WIDTH)
        stores.append(pltpu.make_async_copy(norm_buffer.at[:, i], norm_out.at[:, i], written.at[i]))
        stores[-1].start()
    for copy in started[9:]:
        copy.wait()
    rank = at[5]
    every = grads[...].reshape(WIDTH, COLS)
    total_cols = dot(jnp.ones((8, WIDTH), BF16), every)[0:1]
    row, lane = bias_places(rank, (128, COLS), 1)
    sub = lax.broadcasted_iota(jnp.int32, (128, COLS), 0)
    spots = jnp.where(sub == lane, total_cols, 0.0).astype(BF16)
    for block in range(4):
        rows = slice(block * 256, block * 256 + 256)
        result = columns_step(
            rank, block, xh[rows], columns[rows], hot[rows], total[0:1, rows], every, total_cols, spots
        )
        place, pair = (block % 2) * 8, (block // 2) * 2
        for inside in range(16):
            columns_buffer[place + inside // 2, pair + inside % 2] = result[inside * 16 : inside * 16 + 16]
        here = (slice(place, place + 8), slice(pair, pair + 2))
        stores.append(pltpu.make_async_copy(columns_buffer.at[here], columns_out.at[here], written.at[4 + block]))
        stores[-1].start()
    for copy in stores:
        copy.wait()


def backward(at, *operands):
    remote = pl.BlockSpec(memory_space=pltpu.HBM)
    return pl.pallas_call(
        backward_body,
        out_shape=(token_shape(WIDTH, BF16), jax.ShapeDtypeStruct((16, 4, 16, WIDTH), BF16)),
        in_specs=[smem()] + [remote] * 13 + [pl.BlockSpec(memory_space=pl.ANY)] * 2,
        out_specs=(remote, remote),
        scratch_shapes=[pltpu.VMEM(a.shape, a.dtype) for a in operands[:13]]
        + [
            pltpu.VMEM((2, 4, TOK, COLS), BF16),
            pltpu.VMEM((2, 4, TOK, WIDTH), BF16),
            pltpu.VMEM((16, 4, 16, WIDTH), BF16),
            pltpu.SemaphoreType.DMA((13,)),
            pltpu.SemaphoreType.DMA((8,)),
        ],
        compiler_params=pltpu.CompilerParams(vmem_limit_bytes=VMEM_LIMIT),
        cost_estimate=cost(6 << 30, 16 << 20),
    )(at, *operands)


def tail_grad_body(both, cot, out, total):
    for half in range(2):
        product = tn_dot(both[...], cot[:, half * 512 : half * 512 + 512]).astype(BF16)
        for k in range(8):
            out[2 * k + half, 0:16, :] = product[k * 16 : k * 16 + 16]
            out[2 * k + half, 16:80, :] = product[128 + k * 64 : 192 + k * 64]
    total[...] = dot(jnp.ones((8, WIDTH), BF16), cot[...])


def tail_grad_of(both, cot):
    return pl.pallas_call(
        tail_grad_body,
        out_shape=(jax.ShapeDtypeStruct((16, 80, 512), BF16), jax.ShapeDtypeStruct((8, WIDTH), F32)),
        in_specs=[vmem(), vmem()],
        out_specs=(vmem(), vmem()),
        compiler_params=pltpu.CompilerParams(vmem_limit_bytes=VMEM_LIMIT),
        cost_estimate=cost(2 << 30, 6 << 20),
    )(both, cot)


def rotary_tables():
    position = jnp.arange(256).astype(F32)[:, None]
    lane = jnp.arange(128) % HEAD_DIM
    halves = (lane % (ROT // 2)).astype(F32)
    frequency = jnp.power(10000.0, -2.0 * halves / ROT)[None, :]
    angle = position * frequency
    cosine, sine = jnp.cos(angle), jnp.sin(angle)
    lane = lane[None, :]
    return (
        jnp.where(lane < ROT, cosine, 1.0),
        jnp.where(lane < ROT // 2, -sine, 0.0),
        jnp.where((lane >= ROT // 2) & (lane < ROT), sine, 0.0),
    )


def gather_tokens(block):
    return lax.all_gather(block, GROUP, axis=0, tiled=True)


def scatter_tokens(partial):
    return lax.psum_scatter(partial, GROUP, scatter_dimension=0, tiled=True)


def tail_routes():
    straight, crossed = [], []
    for s in range(2):
        for dp in range(64):
            rank, place = dp // 8, 2 * (dp % 8) + s
            target_dp = (((rank >> 1) & 1) * 16 + place) * 2 + (rank & 1)
            target = (rank >> 2) * 64 + target_dp
            straight.append((s * 64 + dp, target))
            crossed.append(((1 - s) * 64 + dp, target))
    return straight, crossed


def local(
    tokens,
    ln1_gain,
    ln1_bias,
    ln2_gain,
    ln2_bias,
    qkv_weight,
    qkv_bias,
    dense_weight,
    dense_bias,
    fc_in_weight,
    fc_in_bias,
    fc_out_weight,
    fc_out_bias,
    out_grad,
):
    s, yl, z, x, c = (lax.axis_index(a) for a in AXES)
    rank = s * 4 + yl * 2 + c
    at = jnp.stack([s, yl, z, x, c, rank]).astype(jnp.int32)
    straight, crossed = tail_routes()
    shape = jax.ShapeDtypeStruct

    vectors = (ln1_gain, ln1_bias, ln2_gain, ln2_bias, dense_bias, fc_out_bias, qkv_bias, fc_in_bias)
    sent = pack(at, qkv_weight, fc_in_weight, vectors)
    pieces = jnp.stack([sent[0]] + [exchange(sent[d], PAIR, 4, d) for d in range(1, 4)])
    pieces = spread(jnp.broadcast_to(pieces, (16, 4, 16, WIDTH)), PLACES)
    tail = jnp.concatenate([dense_weight, fc_out_weight], axis=0)
    tail = lax.dynamic_slice_in_dim(tail, s * 512, 512, axis=1)
    tail = lax.ppermute(tail, AXES, straight)
    tail = spread(after(jnp.broadcast_to(tail, (16, 80, 512)), pieces), PLACES)

    own_xh = call(norm_body, shape((TOK, WIDTH), BF16), (at, tokens, sent), ordered=True)
    xh = gather_tokens(own_xh)
    cot = gather_tokens(after(out_grad, own_xh))

    xh_tokens, cot_tokens = xh.reshape(2, 4, TOK, WIDTH), cot.reshape(2, 4, TOK, WIDTH)
    tables = rotary_tables()
    rotated, sums, both, slope, turned, columns_in, hot, flipped = forward(at, xh_tokens, pieces, tables)
    tail_grad, total = tail_grad_of(both.reshape(WIDTH, 640), cot)
    mixed_part, tail = mixed_of(both, tail, tail_grad)
    tail_parts = spread(tail_grad, PLACES)
    mixed_sum = scatter_tokens(mixed_part.reshape(WIDTH, WIDTH))
    norm_part, columns_grad = backward(
        at, cot_tokens, tail, rotated, sums, slope, *tables, turned, total, flipped, columns_in, hot, tail_grad, mixed_part
    )
    norm_part, columns_grad = after((norm_part, columns_grad), tail_parts)
    norm_grad = scatter_tokens(norm_part.reshape(WIDTH, WIDTH))
    tail_sum = jnp.sum(tail_parts.astype(F32), axis=0).astype(BF16)
    column_sum = jnp.sum(spread(columns_grad, PLACES).astype(F32), axis=0).astype(BF16)
    column_sum = after(column_sum, mixed_sum)
    parts = spread(jnp.concatenate([column_sum, column_sum], axis=0), GROUP)
    vector = shape((16,), F32)
    mixed, tokens_grad = call(
        outputs_body,
        (shape((TOK, WIDTH), BF16), shape((TOK, WIDTH), F32)),
        (at, tokens, out_grad, norm_grad, mixed_sum, columns_in),
    )
    mine = lax.ppermute(tail_sum, AXES, [(b, a) for a, b in straight])
    other = lax.ppermute(tail_sum, AXES, [(b, a) for a, b in crossed])
    qkv_grad, fc_in_grad, *vectors_grad, dense_grad, fc_out_grad = call(
        owner_body,
        (shape((16, 3 * WIDTH), F32), shape((16, FF), F32))
        + (vector,) * 6
        + (shape((48,), F32), shape((64,), F32), shape((16, WIDTH), F32), shape((64, WIDTH), F32)),
        (at, parts, mine, other, mixed),
        ordered=True,
    )
    g1_grad, b1_grad, g2_grad, b2_grad, bias_grad, same_grad, qb_grad, fb_grad = vectors_grad
    return (
        mixed,
        tokens_grad,
        g1_grad,
        b1_grad,
        g2_grad,
        b2_grad,
        qkv_grad,
        qb_grad,
        dense_grad,
        bias_grad,
        fc_in_grad,
        fb_grad,
        fc_out_grad,
        same_grad,
    )


def solution(mesh):
    grid = Mesh(mesh.devices.reshape(2, 2, 4, 4, 2), AXES)
    rows = P(AXES, None)
    vector = P(AXES[1:])
    matrix = P(AXES[1:], None)
    in_specs = (
        rows,
        vector,
        vector,
        vector,
        vector,
        matrix,
        vector,
        matrix,
        vector,
        matrix,
        vector,
        matrix,
        vector,
        rows,
    )
    out_specs = (
        rows,
        rows,
        vector,
        vector,
        vector,
        vector,
        matrix,
        vector,
        matrix,
        vector,
        matrix,
        vector,
        matrix,
        vector,
    )
    return jax.shard_map(local, mesh=grid, in_specs=in_specs, out_specs=out_specs, check_vma=False)
```

```python
import jax
import jax.numpy as jnp
from jax import lax
from jax.experimental import pallas as pl
from jax.experimental.pallas import tpu as pltpu
from jax.sharding import Mesh
from jax.sharding import PartitionSpec as P

HEADS = 16
HEAD_DIM = 64
ROT = 16
WIDTH = 1024
FF = 4096
TOK = 128
F32 = jnp.float32
BF16 = jnp.bfloat16
EPSILON = 1e-05
AXES = ("s", "yl", "z", "x", "c")
GROUP = ("s", "yl", "c")
PAIR = ("yl", "c")
PLACES = ("z", "x")
QKV = 384
HID = 512
COLS = QKV + HID
COUNTS = (1, 1, 1, 1, 1, 1, 3, 4)
VMEM_LIMIT = 60 * 1024 * 1024


def exchange(values, axes, count, mask):
    return lax.ppermute(values, axes, [(i, i ^ mask) for i in range(count)])


def spread(blocks, axes):
    return lax.all_to_all(blocks, axes, split_axis=0, concat_axis=0, tiled=True)


def after(values, first):
    return lax.optimization_barrier((values, first))[0]


def smem():
    return pl.BlockSpec(memory_space=pltpu.SMEM)


def vmem():
    return pl.BlockSpec(memory_space=pltpu.VMEM)


def call(body, out_shape, operands, ordered=False):
    return pl.pallas_call(
        body,
        out_shape=out_shape,
        in_specs=[smem()] + [vmem()] * (len(operands) - 1 - ordered) + [pl.BlockSpec(memory_space=pl.ANY)] * ordered,
        out_specs=jax.tree.map(lambda _: vmem(), out_shape),
        compiler_params=pltpu.CompilerParams(vmem_limit_bytes=VMEM_LIMIT),
        cost_estimate=pl.CostEstimate(flops=0, bytes_accessed=1 << 10, transcendentals=0),
    )(*operands)


def columns_of(vector, count):
    size = 16 * count
    wide = jnp.broadcast_to(vector[...].astype(F32)[None, :], (16, size))
    row = lax.broadcasted_iota(jnp.int32, (16, size), 0)
    lane = lax.broadcasted_iota(jnp.int32, (16, size), 1)
    return [
        jnp.sum(jnp.where(lane == row * count + i, wide, 0.0), axis=1, keepdims=True) for i in range(count)
    ]


def pack_body(at, *refs):
    vectors, out, copies, done = refs[:10], refs[10], refs[11:21], refs[21]
    qkv, fc_in = copies[8:]
    started = [pltpu.make_async_copy(a, b, done.at[i]) for i, (a, b) in enumerate(zip(vectors, copies))]
    for copy in started:
        copy.start()
    for copy in started:
        copy.wait()
    lane = lax.broadcasted_iota(jnp.int32, (16, 128), 1)
    small = jnp.zeros((16, 128), F32)
    columns = []
    for vector, count in zip(copies, COUNTS):
        columns += columns_of(vector, count)
    for index, column in enumerate(columns):
        small = jnp.where(lane == index, column, small)
    small = small.astype(BF16)
    for d in range(4):
        rank = lax.bitwise_xor(at[5], d)
        parts = []
        for part in range(3):
            first = pl.multiple_of(part * WIDTH + rank * 128, 128)
            parts.append(qkv[:, pl.ds(first, 128)])
        parts += [small, fc_in[:, pl.ds(pl.multiple_of(rank * HID, HID), HID)]]
        out[d] = jnp.concatenate(parts, axis=1)


def pack(at, qkv_weight, fc_in_weight, vectors):
    anywhere = pl.BlockSpec(memory_space=pltpu.HBM)
    return pl.pallas_call(
        pack_body,
        out_shape=jax.ShapeDtypeStruct((4, 16, WIDTH), BF16),
        in_specs=[smem()] + [anywhere] * 10,
        out_specs=vmem(),
        scratch_shapes=[pltpu.VMEM((16 * count,), BF16) for count in COUNTS]
        + [pltpu.VMEM((16, 3 * WIDTH), BF16), pltpu.VMEM((16, FF), BF16), pltpu.SemaphoreType.DMA((10,))],
        compiler_params=pltpu.CompilerParams(vmem_limit_bytes=VMEM_LIMIT),
        cost_estimate=cost(0, 0),
    )(at, *vectors, qkv_weight, fc_in_weight)


def norm_stats(tokens):
    inputs = tokens[...].astype(F32)
    centered = inputs - jnp.mean(inputs, axis=1, keepdims=True)
    inverse = lax.rsqrt(jnp.mean(centered * centered, axis=1, keepdims=True) + EPSILON)
    return inputs, centered * inverse, inverse


def norm_body(at, tokens, ahead, out):
    out[...] = norm_stats(tokens)[1].astype(BF16)


def outputs_body(at, tokens, out_grad, norm_grad, mixed_sum, columns, mixed, tokens_grad):
    inputs, normed, inverse = norm_stats(tokens)
    sel = lax.broadcasted_iota(jnp.int32, (8, 128), 1)
    sel = jnp.where((sel == 4) | (sel == 5), 1.0, 0.0).astype(BF16)
    bias = nt_dot(sel, columns[:, QKV:512])[0:1]
    mixed[...] = (inputs + mixed_sum[...].astype(F32) + bias).astype(BF16)
    grad = norm_grad[...].astype(F32)
    mean_grad = jnp.mean(grad, axis=1, keepdims=True)
    mean_dot = jnp.mean(grad * normed, axis=1, keepdims=True)
    tokens_grad[...] = out_grad[...].astype(F32) + inverse * (grad - mean_grad - normed * mean_dot)


def owner_body(at, *refs):
    pieces, mine, other, ahead = refs[:4]
    (qkv_out, in_out, g1, b1, g2, b2, bias, same, qb, fb, dense_out, fc_out) = refs[4:]
    for half, part in ((at[0], mine), (1 - at[0], other)):
        lanes = pl.ds(pl.multiple_of(half * 512, 512), 512)
        dense_out[:, lanes] = part[0:16].astype(F32)
        fc_out[:, lanes] = part[16:80].astype(F32)
    small = jnp.zeros((16, 128), F32)
    for rank in range(8):
        block = pieces[rank]
        for part in range(3):
            first = part * WIDTH + rank * 128
            qkv_out[:, first : first + 128] = block[:, part * 128 : part * 128 + 128].astype(F32)
        small = small + block[:, QKV:512].astype(F32)
        in_out[:, rank * HID : rank * HID + HID] = block[:, 512:].astype(F32)
    lane = 0
    for vector, count in ((g1, 1), (b1, 1), (g2, 1), (b2, 1), (bias, 1), (None, 1), (qb, 3), (fb, 4)):
        if vector is not None:
            size = 16 * count
            row = lax.broadcasted_iota(jnp.int32, (16, size), 0)
            place = lax.broadcasted_iota(jnp.int32, (16, size), 1)
            total = jnp.zeros((16, size), F32)
            for i in range(count):
                total = jnp.where(place == row * count + i, small[:, lane + i : lane + i + 1], total)
            vector[...] = jnp.sum(total, axis=0)
            if vector is bias:
                same[...] = jnp.sum(total, axis=0)
        lane += count


def nt_dot(left, right):
    return lax.dot_general(left, right, (((1,), (1,)), ((), ())), preferred_element_type=F32)


def tn_dot(left, right):
    return lax.dot_general(left, right, (((0,), (0,)), ((), ())), preferred_element_type=F32)


def dot(left, right):
    return jnp.dot(left, right, preferred_element_type=F32)


def bias_places(rank, shape, dim):
    column = lax.broadcasted_iota(jnp.int32, shape, dim)
    part, within = lax.shift_right_logical(column, 7), lax.bitwise_and(column, 127)
    q_column = part * WIDTH + rank * 128 + within
    h_column = rank * HID + column - QKV
    q_row = lax.div(q_column, 3)
    is_q = column < QKV
    row = jnp.where(is_q, q_row, lax.shift_right_logical(h_column, 2))
    lane = jnp.where(is_q, 6 + q_column - 3 * q_row, 9 + lax.bitwise_and(h_column, 3))
    return row, lane


def turn(values, cosine, low, high, sign):
    back = pltpu.roll(values, 128 - 8, 1)
    ahead = pltpu.roll(values, 8, 1)
    return values * cosine + sign * (back * low + ahead * high)


def causal():
    row = lax.broadcasted_iota(jnp.int32, (256, 256), 0)
    return row >= lax.broadcasted_iota(jnp.int32, (256, 256), 1)


def owner_rows(at, place, d):
    pair = lax.bitwise_xor(at[1] * 2 + at[4], d)
    return pl.multiple_of((lax.shift_right_logical(pair, 1) * 16 + place) * 32 + lax.bitwise_and(pair, 1) * 16, 16)


def forward_body(at, xh, pieces, cos, sin_low, sin_high, rotated, sums, both, slope, turned, columns, hot, flipped, scaled, bias):
    rank = at[5]

    @pl.when(pl.program_id(0) == 0)
    def _():
        for place in range(16):
            for d in range(4):
                columns[pl.ds(owner_rows(at, place, d), 16), :] = pieces[place, d]
        params = columns[:, QKV:512]
        weights = jnp.concatenate([columns[:, :QKV], columns[:, 512:]], axis=1)
        row, lane = bias_places(rank, (WIDTH, COLS), 1)
        hot[...] = (lax.broadcasted_iota(jnp.int32, (WIDTH, COLS), 0) == row).astype(F32).astype(BF16)
        row, lane = bias_places(rank, (128, COLS), 1)
        sub = lax.broadcasted_iota(jnp.int32, (128, COLS), 0)
        column = lax.broadcasted_iota(jnp.int32, (128, COLS), 1)
        own = jnp.where(sub == lane, tn_dot(params, hot[...]), 0.0)
        shifted = jnp.where(sub == jnp.where(column < QKV, 1, 3), tn_dot(params, weights), 0.0)
        bias[...] = jnp.sum(own + shifted, axis=0, keepdims=True)
        gains = params.astype(F32)
        scaled[:, :QKV] = (weights[:, :QKV].astype(F32) * gains[:, 0:1]).astype(BF16)
        scaled[:, QKV:] = (weights[:, QKV:].astype(F32) * gains[:, 2:3]).astype(BF16)
        turned[...] = scaled[...].T

    tokens = xh[...].reshape(256, WIDTH)
    for piece in range(2):
        first = pl.multiple_of(piece * 512 + pl.program_id(0) * TOK, TOK)
        flipped[:, pl.ds(first, TOK)] = tokens[piece * TOK : piece * TOK + TOK].T
    proj = dot(tokens, scaled[:, :QKV]) + bias[:, :QKV]
    table = cos[...], sin_low[...], sin_high[...]
    queries = turn(proj[:, 0:128], *table, 1.0).astype(BF16)
    keys = turn(proj[:, 128:256], *table, 1.0).astype(BF16)
    values = proj[:, 256:384].astype(BF16)
    rotated[...] = jnp.concatenate([queries, keys, values], axis=1).reshape(rotated.shape)
    allowed = causal()
    outs, logs = [], []
    for h in range(2):
        lanes = slice(h * HEAD_DIM, (h + 1) * HEAD_DIM)
        scores = jnp.where(allowed, nt_dot(queries[:, lanes], keys[:, lanes]) * HEAD_DIM ** (-0.5), -1e30)
        peak = jnp.max(scores, axis=1, keepdims=True)
        weights = jnp.exp(scores - peak)
        norm = jnp.sum(weights, axis=1, keepdims=True)
        outs.append(dot((weights / norm).astype(BF16), values[:, lanes]))
        logs.append(jnp.broadcast_to(peak + jnp.log(norm), (256, HEAD_DIM)))
    sums[...] = jnp.concatenate(logs, axis=1).reshape(sums.shape)
    attended = jnp.concatenate(outs, axis=1).astype(BF16)
    hidden = dot(tokens, scaled[:, QKV:]) + bias[:, QKV:]
    cdf = 0.5 * (1.0 + lax.erf(hidden * (0.5**0.5)))
    both[...] = jnp.concatenate([attended, (hidden * cdf).astype(BF16)], axis=1).reshape(both.shape)
    slope[...] = (cdf + hidden * jnp.exp(-0.5 * hidden * hidden) * 0.3989422804014327).astype(BF16).reshape(slope.shape)


def token_spec(lanes):
    return pl.BlockSpec((2, 1, TOK, lanes), lambda i: (0, i, 0, 0))


def token_shape(lanes, dtype):
    return jax.ShapeDtypeStruct((2, 4, TOK, lanes), dtype)


def whole(rows, lanes):
    return pl.BlockSpec((rows, lanes), lambda i: (0, 0))


def cost(flops, size):
    return pl.CostEstimate(flops=flops >> 10, bytes_accessed=size >> 10, transcendentals=0)


def forward(at, xh, pieces, tables):
    table = whole(256, 128)
    return pl.pallas_call(
        forward_body,
        grid=(4,),
        out_shape=(
            token_shape(QKV, BF16),
            token_shape(128, F32),
            token_shape(128 + HID, BF16),
            token_shape(HID, BF16),
            jax.ShapeDtypeStruct((COLS, WIDTH), BF16),
            jax.ShapeDtypeStruct((WIDTH, WIDTH), BF16),
            jax.ShapeDtypeStruct((WIDTH, COLS), BF16),
            jax.ShapeDtypeStruct((WIDTH, WIDTH), BF16),
        ),
        in_specs=[
            smem(),
            token_spec(WIDTH),
            pl.BlockSpec((16, 4, 16, WIDTH), lambda i: (0, 0, 0, 0)),
            table,
            table,
            table,
        ],
        out_specs=(
            token_spec(QKV),
            token_spec(128),
            token_spec(128 + HID),
            token_spec(HID),
            whole(COLS, WIDTH),
            whole(WIDTH, WIDTH),
            whole(WIDTH, COLS),
            whole(WIDTH, WIDTH),
        ),
        scratch_shapes=[pltpu.VMEM((WIDTH, COLS), BF16), pltpu.VMEM((1, COLS), F32)],
        compiler_params=pltpu.CompilerParams(vmem_limit_bytes=VMEM_LIMIT),
        cost_estimate=cost(4 << 30, 8 << 20),
    )(at, xh, pieces, *tables)


def assemble(blocks, tail):
    for place in range(16):
        k, lane = place // 2, (place % 2) * 512
        tail[k * 16 : k * 16 + 16, lane : lane + 512] = blocks[place, 0:16, :]
        tail[128 + k * 64 : 192 + k * 64, lane : lane + 512] = blocks[place, 16:80, :]


def mixed_body(both, blocks, ahead, out_ref, both_here, blocks_here, tail, buffer, done, written):
    started = fetch((blocks, both), (blocks_here, both_here), done)
    started[0].wait()
    assemble(blocks_here, tail)
    started[1].wait()
    stores = []
    for i in range(4):
        product = dot(both_here[:, i].reshape(256, 128 + HID), tail[...])
        buffer[:, i] = product.astype(BF16).reshape(2, TOK, WIDTH)
        stores.append(pltpu.make_async_copy(buffer.at[:, i], out_ref.at[:, i], written.at[i]))
        stores[-1].start()
    for copy in stores:
        copy.wait()


def mixed_of(both, blocks, ahead):
    remote = pl.BlockSpec(memory_space=pltpu.HBM)
    return pl.pallas_call(
        mixed_body,
        out_shape=token_shape(WIDTH, BF16),
        in_specs=[pl.BlockSpec(memory_space=pl.ANY)] * 3,
        out_specs=remote,
        scratch_shapes=[
            pltpu.VMEM(both.shape, BF16),
            pltpu.VMEM(blocks.shape, BF16),
            pltpu.VMEM((640, WIDTH), BF16),
            pltpu.VMEM((2, 4, TOK, WIDTH), BF16),
            pltpu.SemaphoreType.DMA((2,)),
            pltpu.SemaphoreType.DMA((4,)),
        ],
        compiler_params=pltpu.CompilerParams(vmem_limit_bytes=VMEM_LIMIT),
        cost_estimate=cost(2 << 30, 6 << 20),
    )(both, blocks, ahead)


def sequence_step(packed, logs, slope, cotangent, tail, table):
    grad = dot(cotangent, tail[:, :128]).astype(BF16)
    dhid = (dot(cotangent, tail[:, 128:]) * slope.astype(F32)).astype(BF16)
    allowed = causal()
    dqs, dks, dvs = [], [], []
    scale = HEAD_DIM ** (-0.5)
    for h in range(2):
        q, k, v = (packed[:, i * 128 + h * HEAD_DIM : i * 128 + (h + 1) * HEAD_DIM] for i in range(3))
        g = grad[:, h * HEAD_DIM : (h + 1) * HEAD_DIM]
        scores = nt_dot(q, k) * scale - logs[:, h * HEAD_DIM : h * HEAD_DIM + 1]
        probs = jnp.exp(jnp.where(allowed, scores, -1e30))
        dprobs = nt_dot(g, v)
        inner = jnp.sum(probs * dprobs, axis=1, keepdims=True)
        ds = (probs * (dprobs - inner)).astype(BF16)
        dqs.append(dot(ds, k) * scale)
        dks.append(tn_dot(ds, q) * scale)
        dvs.append(tn_dot(probs.astype(BF16), g))
    dq = turn(jnp.concatenate(dqs, axis=1).astype(BF16).astype(F32), *table, -1.0)
    dk = turn(jnp.concatenate(dks, axis=1).astype(BF16).astype(F32), *table, -1.0)
    dv = jnp.concatenate(dvs, axis=1)
    back = jnp.concatenate([dq.astype(BF16), dk.astype(BF16), dv.astype(BF16), dhid], axis=1)
    return back


def columns_step(rank, block, xh, columns, hot, total, grads, total_cols, spots):
    product = dot(xh, grads)
    params = columns[:, QKV:512].astype(F32)
    weights = jnp.concatenate([columns[:, :QKV], columns[:, 512:]], axis=1).astype(F32)
    small = nt_dot(hot, spots)
    lane = lax.broadcasted_iota(jnp.int32, (256, 128), 1)
    mirror = lax.broadcasted_iota(jnp.int32, (256, 256), 0) == lax.broadcasted_iota(jnp.int32, (256, 256), 1)
    mine = jnp.sum(jnp.where(mirror, total, 0.0), axis=1, keepdims=True)
    small = jnp.where((lane == 4) & (rank == 0), mine, small)
    changes = []
    for first, last, index in ((0, QKV, 0), (QKV, COLS, 2)):
        w, g, t = weights[:, first:last], product[:, first:last], total_cols[:, first:last]
        small = jnp.where(lane == index, jnp.sum(w * g, axis=1, keepdims=True), small)
        small = jnp.where(lane == index + 1, jnp.sum(w * t, axis=1, keepdims=True), small)
        change = (params[:, index : index + 1] * g + params[:, index + 1 : index + 2] * t).astype(BF16)
        changes.append(change)
    return jnp.concatenate([changes[0], small.astype(BF16), changes[1]], axis=1)


def fetch(sources, copies, done):
    started = [pltpu.make_async_copy(a, b, done.at[i]) for i, (a, b) in enumerate(zip(sources, copies))]
    for copy in started:
        copy.start()
    return started


def backward_body(at, *refs):
    sources, (norm_out, columns_out), copies = refs[:13], refs[15:17], refs[17:30]
    grads, norm_buffer, columns_buffer, weights, done, written = refs[30:]
    cot, blocks, rotated, sums, slope, cos, sin_low, sin_high, scaled, total, xh, columns, hot = copies
    started = fetch(sources, copies, done)
    for copy in started[:8]:
        copy.wait()
    assemble(blocks, weights)
    tail = weights[...].T
    table = cos[...], sin_low[...], sin_high[...]
    stores = []
    for i in range(4):
        back = sequence_step(
            rotated[:, i].reshape(256, QKV),
            sums[:, i].reshape(256, 128),
            slope[:, i].reshape(256, HID),
            cot[:, i].reshape(256, WIDTH),
            tail,
            table,
        )
        grads[:, i] = back.reshape(2, TOK, COLS)
        if i == 0:
            started[8].wait()
        norm_buffer[:, i] = dot(back, scaled[...]).astype(BF16).reshape(2, TOK, WIDTH)
        stores.append(pltpu.make_async_copy(norm_buffer.at[:, i], norm_out.at[:, i], written.at[i]))
        stores[-1].start()
    for copy in started[9:]:
        copy.wait()
    rank = at[5]
    every = grads[...].reshape(WIDTH, COLS)
    total_cols = dot(jnp.ones((8, WIDTH), BF16), every)[0:1]
    row, lane = bias_places(rank, (128, COLS), 1)
    sub = lax.broadcasted_iota(jnp.int32, (128, COLS), 0)
    spots = jnp.where(sub == lane, total_cols, 0.0).astype(BF16)
    for block in range(4):
        rows = slice(block * 256, block * 256 + 256)
        result = columns_step(
            rank, block, xh[rows], columns[rows], hot[rows], total[0:1, rows], every, total_cols, spots
        )
        place, pair = (block % 2) * 8, (block // 2) * 2
        for inside in range(16):
            columns_buffer[place + inside // 2, pair + inside % 2] = result[inside * 16 : inside * 16 + 16]
        here = (slice(place, place + 8), slice(pair, pair + 2))
        stores.append(pltpu.make_async_copy(columns_buffer.at[here], columns_out.at[here], written.at[4 + block]))
        stores[-1].start()
    for copy in stores:
        copy.wait()


def backward(at, *operands):
    remote = pl.BlockSpec(memory_space=pltpu.HBM)
    return pl.pallas_call(
        backward_body,
        out_shape=(token_shape(WIDTH, BF16), jax.ShapeDtypeStruct((16, 4, 16, WIDTH), BF16)),
        in_specs=[smem()] + [pl.BlockSpec(memory_space=pl.ANY)] * 15,
        out_specs=(remote, remote),
        scratch_shapes=[pltpu.VMEM(a.shape, a.dtype) for a in operands[:13]]
        + [
            pltpu.VMEM((2, 4, TOK, COLS), BF16),
            pltpu.VMEM((2, 4, TOK, WIDTH), BF16),
            pltpu.VMEM((16, 4, 16, WIDTH), BF16),
            pltpu.VMEM((640, WIDTH), BF16),
            pltpu.SemaphoreType.DMA((13,)),
            pltpu.SemaphoreType.DMA((8,)),
        ],
        compiler_params=pltpu.CompilerParams(vmem_limit_bytes=VMEM_LIMIT),
        cost_estimate=cost(6 << 30, 16 << 20),
    )(at, *operands)


def tail_grad_body(both, cot, out, total):
    for half in range(2):
        product = tn_dot(both[...], cot[:, half * 512 : half * 512 + 512]).astype(BF16)
        for k in range(8):
            out[2 * k + half, 0:16, :] = product[k * 16 : k * 16 + 16]
            out[2 * k + half, 16:80, :] = product[128 + k * 64 : 192 + k * 64]
    total[...] = dot(jnp.ones((8, WIDTH), BF16), cot[...])


def tail_grad_of(both, cot):
    return pl.pallas_call(
        tail_grad_body,
        out_shape=(jax.ShapeDtypeStruct((16, 80, 512), BF16), jax.ShapeDtypeStruct((8, WIDTH), F32)),
        in_specs=[vmem(), vmem()],
        out_specs=(vmem(), vmem()),
        compiler_params=pltpu.CompilerParams(vmem_limit_bytes=VMEM_LIMIT),
        cost_estimate=cost(2 << 30, 6 << 20),
    )(both, cot)


def rotary_tables():
    position = jnp.arange(256).astype(F32)[:, None]
    lane = jnp.arange(128) % HEAD_DIM
    halves = (lane % (ROT // 2)).astype(F32)
    frequency = jnp.power(10000.0, -2.0 * halves / ROT)[None, :]
    angle = position * frequency
    cosine, sine = jnp.cos(angle), jnp.sin(angle)
    lane = lane[None, :]
    return (
        jnp.where(lane < ROT, cosine, 1.0),
        jnp.where(lane < ROT // 2, -sine, 0.0),
        jnp.where((lane >= ROT // 2) & (lane < ROT), sine, 0.0),
    )


def gather_tokens(block):
    return lax.all_gather(block, GROUP, axis=0, tiled=True)


def scatter_tokens(partial):
    return lax.psum_scatter(partial, GROUP, scatter_dimension=0, tiled=True)


def tail_routes():
    straight, crossed = [], []
    for s in range(2):
        for dp in range(64):
            rank, place = dp // 8, 2 * (dp % 8) + s
            target_dp = (((rank >> 1) & 1) * 16 + place) * 2 + (rank & 1)
            target = (rank >> 2) * 64 + target_dp
            straight.append((s * 64 + dp, target))
            crossed.append(((1 - s) * 64 + dp, target))
    return straight, crossed


def local(
    tokens,
    ln1_gain,
    ln1_bias,
    ln2_gain,
    ln2_bias,
    qkv_weight,
    qkv_bias,
    dense_weight,
    dense_bias,
    fc_in_weight,
    fc_in_bias,
    fc_out_weight,
    fc_out_bias,
    out_grad,
):
    s, yl, z, x, c = (lax.axis_index(a) for a in AXES)
    rank = s * 4 + yl * 2 + c
    at = jnp.stack([s, yl, z, x, c, rank]).astype(jnp.int32)
    straight, crossed = tail_routes()
    shape = jax.ShapeDtypeStruct

    vectors = (ln1_gain, ln1_bias, ln2_gain, ln2_bias, dense_bias, fc_out_bias, qkv_bias, fc_in_bias)
    sent = pack(at, qkv_weight, fc_in_weight, vectors)
    pieces = jnp.stack([sent[0]] + [exchange(sent[d], PAIR, 4, d) for d in range(1, 4)])
    pieces = spread(jnp.broadcast_to(pieces, (16, 4, 16, WIDTH)), PLACES)
    tail = jnp.concatenate([dense_weight, fc_out_weight], axis=0)
    tail = lax.dynamic_slice_in_dim(tail, s * 512, 512, axis=1)
    tail = lax.ppermute(tail, AXES, straight)
    tail = spread(after(jnp.broadcast_to(tail, (16, 80, 512)), pieces), PLACES)

    own_xh = call(norm_body, shape((TOK, WIDTH), BF16), (at, tokens, sent), ordered=True)
    xh = gather_tokens(own_xh)
    cot = gather_tokens(after(out_grad, own_xh))

    xh_tokens, cot_tokens = xh.reshape(2, 4, TOK, WIDTH), cot.reshape(2, 4, TOK, WIDTH)
    tables = rotary_tables()
    rotated, sums, both, slope, turned, columns_in, hot, flipped = forward(at, xh_tokens, pieces, tables)
    tail_grad, total = tail_grad_of(both.reshape(WIDTH, 640), cot)
    mixed_part = mixed_of(both, tail, tail_grad)
    tail_parts = spread(tail_grad, PLACES)
    mixed_sum = scatter_tokens(mixed_part.reshape(WIDTH, WIDTH))
    norm_part, columns_grad = backward(
        at, cot_tokens, tail, rotated, sums, slope, *tables, turned, total, flipped, columns_in, hot, tail_grad, tail_grad
    )
    norm_part, columns_grad = after((norm_part, columns_grad), tail_parts)
    norm_grad = scatter_tokens(norm_part.reshape(WIDTH, WIDTH))
    column_sum = jnp.sum(spread(columns_grad, PLACES).astype(F32), axis=0).astype(BF16)
    tail_sum = jnp.sum(tail_parts.astype(F32), axis=0).astype(BF16)
    mine = lax.ppermute(tail_sum, AXES, [(b, a) for a, b in straight])
    other = lax.ppermute(tail_sum, AXES, [(b, a) for a, b in crossed])
    column_sum = after(column_sum, (mixed_sum, mine, other))
    parts = spread(jnp.concatenate([column_sum, column_sum], axis=0), GROUP)
    vector = shape((16,), F32)
    mixed, tokens_grad = call(
        outputs_body,
        (shape((TOK, WIDTH), BF16), shape((TOK, WIDTH), F32)),
        (at, tokens, out_grad, norm_grad, mixed_sum, columns_in),
    )
    qkv_grad, fc_in_grad, *vectors_grad, dense_grad, fc_out_grad = call(
        owner_body,
        (shape((16, 3 * WIDTH), F32), shape((16, FF), F32))
        + (vector,) * 6
        + (shape((48,), F32), shape((64,), F32), shape((16, WIDTH), F32), shape((64, WIDTH), F32)),
        (at, parts, mine, other, mixed),
        ordered=True,
    )
    g1_grad, b1_grad, g2_grad, b2_grad, bias_grad, same_grad, qb_grad, fb_grad = vectors_grad
    return (
        mixed,
        tokens_grad,
        g1_grad,
        b1_grad,
        g2_grad,
        b2_grad,
        qkv_grad,
        qb_grad,
        dense_grad,
        bias_grad,
        fc_in_grad,
        fb_grad,
        fc_out_grad,
        same_grad,
    )


def solution(mesh):
    grid = Mesh(mesh.devices.reshape(2, 2, 4, 4, 2), AXES)
    rows = P(AXES, None)
    vector = P(AXES[1:])
    matrix = P(AXES[1:], None)
    in_specs = (
        rows,
        vector,
        vector,
        vector,
        vector,
        matrix,
        vector,
        matrix,
        vector,
        matrix,
        vector,
        matrix,
        vector,
        rows,
    )
    out_specs = (
        rows,
        rows,
        vector,
        vector,
        vector,
        vector,
        matrix,
        vector,
        matrix,
        vector,
        matrix,
        vector,
        matrix,
        vector,
    )
    return jax.shard_map(local, mesh=grid, in_specs=in_specs, out_specs=out_specs, check_vma=False)
```

```python
import jax
import jax.numpy as jnp
from jax import lax
from jax.experimental import pallas as pl
from jax.experimental.pallas import tpu as pltpu
from jax.sharding import Mesh
from jax.sharding import PartitionSpec as P

HEADS = 16
HEAD_DIM = 64
ROT = 16
WIDTH = 1024
FF = 4096
TOK = 128
F32 = jnp.float32
BF16 = jnp.bfloat16
EPSILON = 1e-05
AXES = ("s", "yl", "z", "x", "c")
GROUP = ("s", "yl", "c")
PAIR = ("yl", "c")
PLACES = ("z", "x")
QKV = 384
HID = 512
COLS = QKV + HID
COUNTS = (1, 1, 1, 1, 1, 1, 3, 4)
VMEM_LIMIT = 60 * 1024 * 1024


def exchange(values, axes, count, mask):
    return lax.ppermute(values, axes, [(i, i ^ mask) for i in range(count)])


def spread(blocks, axes):
    return lax.all_to_all(blocks, axes, split_axis=0, concat_axis=0, tiled=True)


def after(values, first):
    return lax.optimization_barrier((values, first))[0]


def smem():
    return pl.BlockSpec(memory_space=pltpu.SMEM)


def vmem():
    return pl.BlockSpec(memory_space=pltpu.VMEM)


def call(body, out_shape, operands, ordered=False):
    return pl.pallas_call(
        body,
        out_shape=out_shape,
        in_specs=[smem()] + [vmem()] * (len(operands) - 1 - ordered) + [pl.BlockSpec(memory_space=pl.ANY)] * ordered,
        out_specs=jax.tree.map(lambda _: vmem(), out_shape),
        compiler_params=pltpu.CompilerParams(vmem_limit_bytes=VMEM_LIMIT),
        cost_estimate=pl.CostEstimate(flops=0, bytes_accessed=1 << 10, transcendentals=0),
    )(*operands)


def columns_of(vector, count):
    size = 16 * count
    wide = jnp.broadcast_to(vector[...].astype(F32)[None, :], (16, size))
    row = lax.broadcasted_iota(jnp.int32, (16, size), 0)
    lane = lax.broadcasted_iota(jnp.int32, (16, size), 1)
    return [
        jnp.sum(jnp.where(lane == row * count + i, wide, 0.0), axis=1, keepdims=True) for i in range(count)
    ]


def pack_body(at, *refs):
    vectors, out, copies, done = refs[:10], refs[10], refs[11:21], refs[21]
    qkv, fc_in = copies[8:]
    started = [pltpu.make_async_copy(a, b, done.at[i]) for i, (a, b) in enumerate(zip(vectors, copies))]
    for copy in started:
        copy.start()
    for copy in started:
        copy.wait()
    lane = lax.broadcasted_iota(jnp.int32, (16, 128), 1)
    small = jnp.zeros((16, 128), F32)
    columns = []
    for vector, count in zip(copies, COUNTS):
        columns += columns_of(vector, count)
    for index, column in enumerate(columns):
        small = jnp.where(lane == index + 32 * (at[1] * 2 + at[4]), column, small)
    small = small.astype(BF16)
    for d in range(4):
        rank = lax.bitwise_xor(at[5], d)
        for j in range(7):
            if j < 3:
                first = pl.multiple_of(j * WIDTH + rank * 128, 128)
                out[d, j * 16 : j * 16 + 16] = qkv[:, pl.ds(first, 128)]
            else:
                first = pl.multiple_of(rank * HID + (j - 3) * 128, 128)
                out[d, j * 16 : j * 16 + 16] = fc_in[:, pl.ds(first, 128)]
        out[d, 112:128] = small


def pack(at, qkv_weight, fc_in_weight, vectors):
    anywhere = pl.BlockSpec(memory_space=pltpu.HBM)
    return pl.pallas_call(
        pack_body,
        out_shape=jax.ShapeDtypeStruct((4, 128, 128), BF16),
        in_specs=[smem()] + [anywhere] * 10,
        out_specs=vmem(),
        scratch_shapes=[pltpu.VMEM((16 * count,), BF16) for count in COUNTS]
        + [pltpu.VMEM((16, 3 * WIDTH), BF16), pltpu.VMEM((16, FF), BF16), pltpu.SemaphoreType.DMA((10,))],
        compiler_params=pltpu.CompilerParams(vmem_limit_bytes=VMEM_LIMIT),
        cost_estimate=cost(0, 0),
    )(at, *vectors, qkv_weight, fc_in_weight)


def norm_stats(tokens):
    inputs = tokens[...].astype(F32)
    centered = inputs - jnp.mean(inputs, axis=1, keepdims=True)
    inverse = lax.rsqrt(jnp.mean(centered * centered, axis=1, keepdims=True) + EPSILON)
    return inputs, centered * inverse, inverse


def norm_body(at, tokens, ahead, out):
    out[...] = norm_stats(tokens)[1].astype(BF16)


def outputs_body(at, tokens, out_grad, norm_grad, mixed_sum, columns, mixed, tokens_grad):
    inputs, normed, inverse = norm_stats(tokens)
    sel = lax.broadcasted_iota(jnp.int32, (8, 128), 1)
    sel = jnp.where((sel == 4) | (sel == 5), 1.0, 0.0).astype(BF16)
    bias = nt_dot(sel, columns[:, QKV:512])[0:1]
    mixed[...] = (inputs + mixed_sum[...].astype(F32) + bias).astype(BF16)
    grad = norm_grad[...].astype(F32)
    mean_grad = jnp.mean(grad, axis=1, keepdims=True)
    mean_dot = jnp.mean(grad * normed, axis=1, keepdims=True)
    tokens_grad[...] = out_grad[...].astype(F32) + inverse * (grad - mean_grad - normed * mean_dot)


def owner_body(at, *refs):
    pieces, mine, other, ahead = refs[:4]
    (qkv_out, in_out, g1, b1, g2, b2, bias, same, qb, fb, dense_out, fc_out) = refs[4:]
    for half, part in ((at[0], mine), (1 - at[0], other)):
        lanes = pl.ds(pl.multiple_of(half * 512, 512), 512)
        dense_out[:, lanes] = part[0:16].astype(F32)
        fc_out[:, lanes] = part[16:80].astype(F32)
    small = jnp.zeros((16, 128), F32)
    for rank in range(8):
        block = pieces[rank]
        for part in range(3):
            first = part * WIDTH + rank * 128
            qkv_out[:, first : first + 128] = block[part * 16 : part * 16 + 16].astype(F32)
        small = small + block[112:128].astype(F32)
        for j in range(3, 7):
            first = rank * HID + (j - 3) * 128
            in_out[:, first : first + 128] = block[j * 16 : j * 16 + 16].astype(F32)
    small = pltpu.roll(small, lax.rem(128 - 32 * (at[1] * 2 + at[4]), 128), 1)
    lane = 0
    for vector, count in ((g1, 1), (b1, 1), (g2, 1), (b2, 1), (bias, 1), (None, 1), (qb, 3), (fb, 4)):
        if vector is not None:
            size = 16 * count
            row = lax.broadcasted_iota(jnp.int32, (16, size), 0)
            place = lax.broadcasted_iota(jnp.int32, (16, size), 1)
            total = jnp.zeros((16, size), F32)
            for i in range(count):
                total = jnp.where(place == row * count + i, small[:, lane + i : lane + i + 1], total)
            vector[...] = jnp.sum(total, axis=0)
            if vector is bias:
                same[...] = jnp.sum(total, axis=0)
        lane += count


def nt_dot(left, right):
    return lax.dot_general(left, right, (((1,), (1,)), ((), ())), preferred_element_type=F32)


def tn_dot(left, right):
    return lax.dot_general(left, right, (((0,), (0,)), ((), ())), preferred_element_type=F32)


def dot(left, right):
    return jnp.dot(left, right, preferred_element_type=F32)


def bias_places(rank, shape, dim):
    column = lax.broadcasted_iota(jnp.int32, shape, dim)
    part, within = lax.shift_right_logical(column, 7), lax.bitwise_and(column, 127)
    q_column = part * WIDTH + rank * 128 + within
    h_column = rank * HID + column - QKV
    q_row = lax.div(q_column, 3)
    is_q = column < QKV
    row = jnp.where(is_q, q_row, lax.shift_right_logical(h_column, 2))
    lane = jnp.where(is_q, 6 + q_column - 3 * q_row, 9 + lax.bitwise_and(h_column, 3))
    return row, lane


def turn(values, cosine, low, high, sign):
    back = pltpu.roll(values, 128 - 8, 1)
    ahead = pltpu.roll(values, 8, 1)
    return values * cosine + sign * (back * low + ahead * high)


def causal():
    row = lax.broadcasted_iota(jnp.int32, (256, 256), 0)
    return row >= lax.broadcasted_iota(jnp.int32, (256, 256), 1)


def lane_of(j):
    return j * 128 if j < 3 else j * 128 + 128


def owner_rows(at, place, d):
    pair = lax.bitwise_xor(at[1] * 2 + at[4], d)
    return pl.multiple_of((lax.shift_right_logical(pair, 1) * 16 + place) * 32 + lax.bitwise_and(pair, 1) * 16, 16)


def forward_body(at, xh, pieces, cos, sin_low, sin_high, rotated, sums, both, slope, turned, columns, hot, flipped, scaled, bias):
    rank = at[5]

    @pl.when(pl.program_id(0) == 0)
    def _():
        for place in range(16):
            for d in range(4):
                rows = pl.ds(owner_rows(at, place, d), 16)
                for j in range(7):
                    columns[rows, lane_of(j) : lane_of(j) + 128] = pieces[place, d * 112 + j * 16 : d * 112 + j * 16 + 16]
            folded = pieces[place, 448:464].astype(F32)
            for pair in range(4):
                first = ((pair // 2) * 16 + place) * 32 + (pair % 2) * 16
                own = pltpu.roll(folded, 128 - 32 * pair, 1) if pair else folded
                columns[first : first + 16, QKV:512] = own.astype(BF16)
        params = columns[:, QKV:512]
        weights = jnp.concatenate([columns[:, :QKV], columns[:, 512:]], axis=1)
        row, lane = bias_places(rank, (WIDTH, COLS), 1)
        hot[...] = (lax.broadcasted_iota(jnp.int32, (WIDTH, COLS), 0) == row).astype(F32).astype(BF16)
        row, lane = bias_places(rank, (128, COLS), 1)
        sub = lax.broadcasted_iota(jnp.int32, (128, COLS), 0)
        column = lax.broadcasted_iota(jnp.int32, (128, COLS), 1)
        own = jnp.where(sub == lane, tn_dot(params, hot[...]), 0.0)
        shifted = jnp.where(sub == jnp.where(column < QKV, 1, 3), tn_dot(params, weights), 0.0)
        bias[...] = jnp.sum(own + shifted, axis=0, keepdims=True)
        gains = params.astype(F32)
        scaled[:, :QKV] = (weights[:, :QKV].astype(F32) * gains[:, 0:1]).astype(BF16)
        scaled[:, QKV:] = (weights[:, QKV:].astype(F32) * gains[:, 2:3]).astype(BF16)
        turned[...] = scaled[...].T

    tokens = xh[...].reshape(256, WIDTH)
    for piece in range(2):
        first = pl.multiple_of(piece * 512 + pl.program_id(0) * TOK, TOK)
        flipped[:, pl.ds(first, TOK)] = tokens[piece * TOK : piece * TOK + TOK].T
    proj = dot(tokens, scaled[:, :QKV]) + bias[:, :QKV]
    table = cos[...], sin_low[...], sin_high[...]
    queries = turn(proj[:, 0:128], *table, 1.0).astype(BF16)
    keys = turn(proj[:, 128:256], *table, 1.0).astype(BF16)
    values = proj[:, 256:384].astype(BF16)
    rotated[...] = jnp.concatenate([queries, keys, values], axis=1).reshape(rotated.shape)
    allowed = causal()
    outs, logs = [], []
    for h in range(2):
        lanes = slice(h * HEAD_DIM, (h + 1) * HEAD_DIM)
        scores = jnp.where(allowed, nt_dot(queries[:, lanes], keys[:, lanes]) * HEAD_DIM ** (-0.5), -1e30)
        peak = jnp.max(scores, axis=1, keepdims=True)
        weights = jnp.exp(scores - peak)
        norm = jnp.sum(weights, axis=1, keepdims=True)
        outs.append(dot((weights / norm).astype(BF16), values[:, lanes]))
        logs.append(jnp.broadcast_to(peak + jnp.log(norm), (256, HEAD_DIM)))
    sums[...] = jnp.concatenate(logs, axis=1).reshape(sums.shape)
    attended = jnp.concatenate(outs, axis=1).astype(BF16)
    hidden = dot(tokens, scaled[:, QKV:]) + bias[:, QKV:]
    cdf = 0.5 * (1.0 + lax.erf(hidden * (0.5**0.5)))
    both[...] = jnp.concatenate([attended, (hidden * cdf).astype(BF16)], axis=1).reshape(both.shape)
    slope[...] = (cdf + hidden * jnp.exp(-0.5 * hidden * hidden) * 0.3989422804014327).astype(BF16).reshape(slope.shape)


def token_spec(lanes):
    return pl.BlockSpec((2, 1, TOK, lanes), lambda i: (0, i, 0, 0))


def token_shape(lanes, dtype):
    return jax.ShapeDtypeStruct((2, 4, TOK, lanes), dtype)


def whole(rows, lanes):
    return pl.BlockSpec((rows, lanes), lambda i: (0, 0))


def cost(flops, size):
    return pl.CostEstimate(flops=flops >> 10, bytes_accessed=size >> 10, transcendentals=0)


def forward(at, xh, pieces, tables):
    table = whole(256, 128)
    return pl.pallas_call(
        forward_body,
        grid=(4,),
        out_shape=(
            token_shape(QKV, BF16),
            token_shape(128, F32),
            token_shape(128 + HID, BF16),
            token_shape(HID, BF16),
            jax.ShapeDtypeStruct((COLS, WIDTH), BF16),
            jax.ShapeDtypeStruct((WIDTH, WIDTH), BF16),
            jax.ShapeDtypeStruct((WIDTH, COLS), BF16),
            jax.ShapeDtypeStruct((WIDTH, WIDTH), BF16),
        ),
        in_specs=[
            smem(),
            token_spec(WIDTH),
            pl.BlockSpec((16, 464, 128), lambda i: (0, 0, 0)),
            table,
            table,
            table,
        ],
        out_specs=(
            token_spec(QKV),
            token_spec(128),
            token_spec(128 + HID),
            token_spec(HID),
            whole(COLS, WIDTH),
            whole(WIDTH, WIDTH),
            whole(WIDTH, COLS),
            whole(WIDTH, WIDTH),
        ),
        scratch_shapes=[pltpu.VMEM((WIDTH, COLS), BF16), pltpu.VMEM((1, COLS), F32)],
        compiler_params=pltpu.CompilerParams(vmem_limit_bytes=VMEM_LIMIT),
        cost_estimate=cost(4 << 30, 8 << 20),
    )(at, xh, pieces, *tables)


def assemble(blocks, tail):
    for place in range(16):
        k, lane = place // 2, (place % 2) * 512
        tail[k * 16 : k * 16 + 16, lane : lane + 512] = blocks[place, 0:16, :]
        tail[128 + k * 64 : 192 + k * 64, lane : lane + 512] = blocks[place, 16:80, :]


def mixed_body(both, blocks, ahead, out_ref, both_here, blocks_here, tail, buffer, done, written):
    started = fetch((blocks, both), (blocks_here, both_here), done)
    started[0].wait()
    assemble(blocks_here, tail)
    started[1].wait()
    stores = []
    for i in range(4):
        product = dot(both_here[:, i].reshape(256, 128 + HID), tail[...])
        buffer[:, i] = product.astype(BF16).reshape(2, TOK, WIDTH)
        stores.append(pltpu.make_async_copy(buffer.at[:, i], out_ref.at[:, i], written.at[i]))
        stores[-1].start()
    for copy in stores:
        copy.wait()


def mixed_of(both, blocks, ahead):
    remote = pl.BlockSpec(memory_space=pltpu.HBM)
    return pl.pallas_call(
        mixed_body,
        out_shape=token_shape(WIDTH, BF16),
        in_specs=[pl.BlockSpec(memory_space=pl.ANY)] * 3,
        out_specs=remote,
        scratch_shapes=[
            pltpu.VMEM(both.shape, BF16),
            pltpu.VMEM(blocks.shape, BF16),
            pltpu.VMEM((640, WIDTH), BF16),
            pltpu.VMEM((2, 4, TOK, WIDTH), BF16),
            pltpu.SemaphoreType.DMA((2,)),
            pltpu.SemaphoreType.DMA((4,)),
        ],
        compiler_params=pltpu.CompilerParams(vmem_limit_bytes=VMEM_LIMIT),
        cost_estimate=cost(2 << 30, 6 << 20),
    )(both, blocks, ahead)


def sequence_step(packed, logs, slope, cotangent, tail, table):
    grad = dot(cotangent, tail[:, :128]).astype(BF16)
    dhid = (dot(cotangent, tail[:, 128:]) * slope.astype(F32)).astype(BF16)
    allowed = causal()
    dqs, dks, dvs = [], [], []
    scale = HEAD_DIM ** (-0.5)
    for h in range(2):
        q, k, v = (packed[:, i * 128 + h * HEAD_DIM : i * 128 + (h + 1) * HEAD_DIM] for i in range(3))
        g = grad[:, h * HEAD_DIM : (h + 1) * HEAD_DIM]
        scores = nt_dot(q, k) * scale - logs[:, h * HEAD_DIM : h * HEAD_DIM + 1]
        probs = jnp.exp(jnp.where(allowed, scores, -1e30))
        dprobs = nt_dot(g, v)
        inner = jnp.sum(probs * dprobs, axis=1, keepdims=True)
        ds = (probs * (dprobs - inner)).astype(BF16)
        dqs.append(dot(ds, k) * scale)
        dks.append(tn_dot(ds, q) * scale)
        dvs.append(tn_dot(probs.astype(BF16), g))
    dq = turn(jnp.concatenate(dqs, axis=1).astype(BF16).astype(F32), *table, -1.0)
    dk = turn(jnp.concatenate(dks, axis=1).astype(BF16).astype(F32), *table, -1.0)
    dv = jnp.concatenate(dvs, axis=1)
    back = jnp.concatenate([dq.astype(BF16), dk.astype(BF16), dv.astype(BF16), dhid], axis=1)
    return back


def columns_step(rank, block, xh, columns, hot, total, grads, total_cols, spots):
    product = dot(xh, grads)
    params = columns[:, QKV:512].astype(F32)
    weights = jnp.concatenate([columns[:, :QKV], columns[:, 512:]], axis=1).astype(F32)
    small = nt_dot(hot, spots)
    lane = lax.broadcasted_iota(jnp.int32, (256, 128), 1)
    mirror = lax.broadcasted_iota(jnp.int32, (256, 256), 0) == lax.broadcasted_iota(jnp.int32, (256, 256), 1)
    mine = jnp.sum(jnp.where(mirror, total, 0.0), axis=1, keepdims=True)
    small = jnp.where((lane == 4) & (rank == 0), mine, small)
    changes = []
    for first, last, index in ((0, QKV, 0), (QKV, COLS, 2)):
        w, g, t = weights[:, first:last], product[:, first:last], total_cols[:, first:last]
        small = jnp.where(lane == index, jnp.sum(w * g, axis=1, keepdims=True), small)
        small = jnp.where(lane == index + 1, jnp.sum(w * t, axis=1, keepdims=True), small)
        change = (params[:, index : index + 1] * g + params[:, index + 1 : index + 2] * t).astype(BF16)
        changes.append(change)
    return jnp.concatenate([changes[0], small.astype(BF16), changes[1]], axis=1)


def fetch(sources, copies, done):
    started = [pltpu.make_async_copy(a, b, done.at[i]) for i, (a, b) in enumerate(zip(sources, copies))]
    for copy in started:
        copy.start()
    return started


def backward_body(at, *refs):
    sources, (norm_out, columns_out), copies = refs[:13], refs[15:17], refs[17:30]
    grads, norm_buffer, columns_buffer, weights, done, written = refs[30:]
    cot, blocks, rotated, sums, slope, cos, sin_low, sin_high, scaled, total, xh, columns, hot = copies
    started = fetch(sources, copies, done)
    for copy in started[:8]:
        copy.wait()
    assemble(blocks, weights)
    tail = weights[...].T
    table = cos[...], sin_low[...], sin_high[...]
    stores = []
    for i in range(4):
        back = sequence_step(
            rotated[:, i].reshape(256, QKV),
            sums[:, i].reshape(256, 128),
            slope[:, i].reshape(256, HID),
            cot[:, i].reshape(256, WIDTH),
            tail,
            table,
        )
        grads[:, i] = back.reshape(2, TOK, COLS)
        if i == 0:
            started[8].wait()
        norm_buffer[:, i] = dot(back, scaled[...]).astype(BF16).reshape(2, TOK, WIDTH)
        stores.append(pltpu.make_async_copy(norm_buffer.at[:, i], norm_out.at[:, i], written.at[i]))
        stores[-1].start()
    for copy in started[9:]:
        copy.wait()
    rank = at[5]
    every = grads[...].reshape(WIDTH, COLS)
    total_cols = dot(jnp.ones((8, WIDTH), BF16), every)[0:1]
    row, lane = bias_places(rank, (128, COLS), 1)
    sub = lax.broadcasted_iota(jnp.int32, (128, COLS), 0)
    spots = jnp.where(sub == lane, total_cols, 0.0).astype(BF16)
    for block in range(4):
        rows = slice(block * 256, block * 256 + 256)
        result = columns_step(
            rank, block, xh[rows], columns[rows], hot[rows], total[0:1, rows], every, total_cols, spots
        )
        place, pair = (block % 2) * 8, (block // 2) * 2
        for inside in range(16):
            rows = slice(inside * 16, inside * 16 + 16)
            here, owner = place + inside // 2, pair + inside % 2
            for j in range(7):
                first = owner * 112 + j * 16
                columns_buffer[here, first : first + 16] = result[rows, lane_of(j) : lane_of(j) + 128]
            own = result[rows, QKV:512].astype(F32)
            own = pltpu.roll(own, 32 * owner, 1) if owner else own
            if owner:
                own = own + columns_buffer[here, 448:464].astype(F32)
            columns_buffer[here, 448:464] = own.astype(BF16)
        if block >= 2:
            here = slice(place, place + 8)
            stores.append(pltpu.make_async_copy(columns_buffer.at[here], columns_out.at[here], written.at[2 + block]))
            stores[-1].start()
    for copy in stores:
        copy.wait()


def backward(at, *operands):
    remote = pl.BlockSpec(memory_space=pltpu.HBM)
    return pl.pallas_call(
        backward_body,
        out_shape=(token_shape(WIDTH, BF16), jax.ShapeDtypeStruct((16, 464, 128), BF16)),
        in_specs=[smem()] + [pl.BlockSpec(memory_space=pl.ANY)] * 15,
        out_specs=(remote, remote),
        scratch_shapes=[pltpu.VMEM(a.shape, a.dtype) for a in operands[:13]]
        + [
            pltpu.VMEM((2, 4, TOK, COLS), BF16),
            pltpu.VMEM((2, 4, TOK, WIDTH), BF16),
            pltpu.VMEM((16, 464, 128), BF16),
            pltpu.VMEM((640, WIDTH), BF16),
            pltpu.SemaphoreType.DMA((13,)),
            pltpu.SemaphoreType.DMA((6,)),
        ],
        compiler_params=pltpu.CompilerParams(vmem_limit_bytes=VMEM_LIMIT),
        cost_estimate=cost(6 << 30, 16 << 20),
    )(at, *operands)


def tail_grad_body(both, cot, out, total):
    for half in range(2):
        product = tn_dot(both[...], cot[:, half * 512 : half * 512 + 512]).astype(BF16)
        for k in range(8):
            out[2 * k + half, 0:16, :] = product[k * 16 : k * 16 + 16]
            out[2 * k + half, 16:80, :] = product[128 + k * 64 : 192 + k * 64]
    total[...] = dot(jnp.ones((8, WIDTH), BF16), cot[...])


def tail_grad_of(both, cot):
    return pl.pallas_call(
        tail_grad_body,
        out_shape=(jax.ShapeDtypeStruct((16, 80, 512), BF16), jax.ShapeDtypeStruct((8, WIDTH), F32)),
        in_specs=[vmem(), vmem()],
        out_specs=(vmem(), vmem()),
        compiler_params=pltpu.CompilerParams(vmem_limit_bytes=VMEM_LIMIT),
        cost_estimate=cost(2 << 30, 6 << 20),
    )(both, cot)


def rotary_tables():
    position = jnp.arange(256).astype(F32)[:, None]
    lane = jnp.arange(128) % HEAD_DIM
    halves = (lane % (ROT // 2)).astype(F32)
    frequency = jnp.power(10000.0, -2.0 * halves / ROT)[None, :]
    angle = position * frequency
    cosine, sine = jnp.cos(angle), jnp.sin(angle)
    lane = lane[None, :]
    return (
        jnp.where(lane < ROT, cosine, 1.0),
        jnp.where(lane < ROT // 2, -sine, 0.0),
        jnp.where((lane >= ROT // 2) & (lane < ROT), sine, 0.0),
    )


def gather_tokens(block):
    return lax.all_gather(block, GROUP, axis=0, tiled=True)


def scatter_tokens(partial):
    return lax.psum_scatter(partial, GROUP, scatter_dimension=0, tiled=True)


def tail_routes():
    straight, crossed = [], []
    for s in range(2):
        for dp in range(64):
            rank, place = dp // 8, 2 * (dp % 8) + s
            target_dp = (((rank >> 1) & 1) * 16 + place) * 2 + (rank & 1)
            target = (rank >> 2) * 64 + target_dp
            straight.append((s * 64 + dp, target))
            crossed.append(((1 - s) * 64 + dp, target))
    return straight, crossed


def local(
    tokens,
    ln1_gain,
    ln1_bias,
    ln2_gain,
    ln2_bias,
    qkv_weight,
    qkv_bias,
    dense_weight,
    dense_bias,
    fc_in_weight,
    fc_in_bias,
    fc_out_weight,
    fc_out_bias,
    out_grad,
):
    s, yl, z, x, c = (lax.axis_index(a) for a in AXES)
    rank = s * 4 + yl * 2 + c
    at = jnp.stack([s, yl, z, x, c, rank]).astype(jnp.int32)
    straight, crossed = tail_routes()
    shape = jax.ShapeDtypeStruct

    vectors = (ln1_gain, ln1_bias, ln2_gain, ln2_bias, dense_bias, fc_out_bias, qkv_bias, fc_in_bias)
    sent = pack(at, qkv_weight, fc_in_weight, vectors)
    pieces = jnp.stack([sent[0]] + [exchange(sent[d], PAIR, 4, d) for d in range(1, 4)])
    folded = pieces[0, 112:] + pieces[1, 112:] + pieces[2, 112:] + pieces[3, 112:]
    pieces = jnp.concatenate([pieces[:, :112].reshape(448, 128), folded], axis=0)
    pieces = spread(jnp.broadcast_to(pieces, (16, 464, 128)), PLACES)
    tail = jnp.concatenate([dense_weight, fc_out_weight], axis=0)
    tail = lax.dynamic_slice_in_dim(tail, s * 512, 512, axis=1)
    tail = lax.ppermute(tail, AXES, straight)
    tail = spread(after(jnp.broadcast_to(tail, (16, 80, 512)), pieces), PLACES)

    own_xh = call(norm_body, shape((TOK, WIDTH), BF16), (at, tokens, sent), ordered=True)
    xh = gather_tokens(own_xh)
    cot = gather_tokens(after(out_grad, own_xh))

    xh_tokens, cot_tokens = xh.reshape(2, 4, TOK, WIDTH), cot.reshape(2, 4, TOK, WIDTH)
    tables = rotary_tables()
    rotated, sums, both, slope, turned, columns_in, hot, flipped = forward(at, xh_tokens, pieces, tables)
    tail_grad, total = tail_grad_of(both.reshape(WIDTH, 640), cot)
    mixed_part = mixed_of(both, tail, tail_grad)
    tail_parts = spread(tail_grad, PLACES)
    mixed_sum = scatter_tokens(mixed_part.reshape(WIDTH, WIDTH))
    norm_part, columns_grad = backward(
        at, cot_tokens, tail, rotated, sums, slope, *tables, turned, total, flipped, columns_in, hot, tail_grad, tail_grad
    )
    norm_part, columns_grad = after((norm_part, columns_grad), tail_parts)
    norm_grad = scatter_tokens(norm_part.reshape(WIDTH, WIDTH))
    column_sum = jnp.sum(spread(columns_grad, PLACES).astype(F32), axis=0).astype(BF16)
    tail_sum = jnp.sum(tail_parts.astype(F32), axis=0).astype(BF16)
    mine = lax.ppermute(tail_sum, AXES, [(b, a) for a, b in straight])
    other = lax.ppermute(tail_sum, AXES, [(b, a) for a, b in crossed])
    column_sum = after(column_sum, (mixed_sum, mine, other))
    small_sum = jnp.broadcast_to(column_sum[448:], (4, 16, 128))
    column_sum = jnp.concatenate([column_sum[:448].reshape(4, 112, 128), small_sum], axis=1)
    parts = spread(jnp.concatenate([column_sum, column_sum], axis=0), GROUP)
    vector = shape((16,), F32)
    mixed, tokens_grad = call(
        outputs_body,
        (shape((TOK, WIDTH), BF16), shape((TOK, WIDTH), F32)),
        (at, tokens, out_grad, norm_grad, mixed_sum, columns_in),
    )
    qkv_grad, fc_in_grad, *vectors_grad, dense_grad, fc_out_grad = call(
        owner_body,
        (shape((16, 3 * WIDTH), F32), shape((16, FF), F32))
        + (vector,) * 6
        + (shape((48,), F32), shape((64,), F32), shape((16, WIDTH), F32), shape((64, WIDTH), F32)),
        (at, parts, mine, other, mixed),
        ordered=True,
    )
    g1_grad, b1_grad, g2_grad, b2_grad, bias_grad, same_grad, qb_grad, fb_grad = vectors_grad
    return (
        mixed,
        tokens_grad,
        g1_grad,
        b1_grad,
        g2_grad,
        b2_grad,
        qkv_grad,
        qb_grad,
        dense_grad,
        bias_grad,
        fc_in_grad,
        fb_grad,
        fc_out_grad,
        same_grad,
    )


def solution(mesh):
    grid = Mesh(mesh.devices.reshape(2, 2, 4, 4, 2), AXES)
    rows = P(AXES, None)
    vector = P(AXES[1:])
    matrix = P(AXES[1:], None)
    in_specs = (
        rows,
        vector,
        vector,
        vector,
        vector,
        matrix,
        vector,
        matrix,
        vector,
        matrix,
        vector,
        matrix,
        vector,
        rows,
    )
    out_specs = (
        rows,
        rows,
        vector,
        vector,
        vector,
        vector,
        matrix,
        vector,
        matrix,
        vector,
        matrix,
        vector,
        matrix,
        vector,
    )
    return jax.shard_map(local, mesh=grid, in_specs=in_specs, out_specs=out_specs, check_vma=False)
```
